128 devices in a mesh: box: 16 (over y, x_hi, core), blk: 8 (over x_lo, z).
Axes of the slice: x: 4 (x_hi: 2, x_lo: 2; x = x_hi * 2 + x_lo), y: 4, z: 4, core: 2. Of those that a mesh axis runs over, the one named last changes fastest.
Arguments:
- interface_rows: float32 [2, 16, 256, 1024], P(None, 'box', 'blk'), as said below
- exterior_rows: float32 [2, 16, 768, 1024], P(None, 'box', 'blk'), as said below
- pml_mask: int32 [2, 16, 1024], P(None, 'box'), may hold values 0 or 1
Outputs:
- level_one: float32 [2, 16, 768, 1536], P(None, 'box', 'blk')
- level_two: float32 [2, 16, 384, 1536], P(None, 'box', 'blk')
The draws below stay inside these ranges and needn't reach their ends.
Inputs may be any that keep to these rules, and one draw needn't show every extreme that they name: `interface_rows`: for every slot and leaf, the matrix formed by its interface rows above its exterior rows is symmetric and positive definite. `exterior_rows`: for every slot and leaf, the matrix formed by its interface rows above its exterior rows is symmetric and positive definite.
All inputs are finite; a program needn't handle non-finite values. No bound on the sum of `pml_mask` on one device may be relied on, other than what follows from the above.
Results may differ from the reference program's by a relative error of at most 0.00005.
Values sent between devices are 32-bit elements; how exact they have to be, the bound alone decides.
No kernel may reach another device: no remote copies, remote signals or barrier semaphores. Data moves between devices by JAX's collectives and lax.ppermute only.
A program may use at most 128 MiB of HBM per device.

```python
import math
import jax
import jax.numpy as jnp
from jax import lax

M = 1024
K = 256
SEGMENT = 16
SLOTS = 2
R = 768
BOXES = 16


def full_matrix(key, log_spread):
    jitter = jax.random.uniform(key, (SLOTS, BOXES, M), jnp.float32, -0.3, 0.3)
    places = jnp.arange(M, dtype=jnp.float32) + jitter
    distance = jnp.abs(places[..., :, None] - places[..., None, :])
    distance = jnp.minimum(distance, M - distance)
    kernel = jnp.exp(-distance / (M / 16.0))
    diagonal_gain = jax.random.uniform(jax.random.fold_in(key, 11), (SLOTS, BOXES, M), jnp.float32, 1.0, 2.0)
    scaling = jnp.exp(log_spread * jax.random.uniform(jax.random.fold_in(key, 12), (SLOTS, BOXES, M), jnp.float32, 0.0, 1.0))
    entries = jax.random.uniform(jax.random.fold_in(key, 13), (SLOTS, BOXES, M, M), jnp.float32, -1.0, 1.0)
    coupling = (entries + jnp.swapaxes(entries, -1, -2)) * (0.6 / math.sqrt(2.0 * M))
    identity = jnp.eye(M, dtype=jnp.float32)
    matrix = kernel + coupling + identity * diagonal_gain[..., :, None]
    return matrix * scaling[..., :, None] * scaling[..., None, :]


def draw_interface_rows(key, part):
    matrix = full_matrix(key, math.log(1.5))
    return matrix[:, :, :K, :]


def draw_exterior_rows(key, part):
    matrix = full_matrix(key, math.log(1.5))
    return matrix[:, :, K:, :]


def set_ends(drawn, own_key, low, high):
    extent = drawn.shape
    spot = [jax.random.randint(jax.random.fold_in(own_key, axis), (), 0, extent[axis]) for axis in range(len(extent))]
    drawn = drawn.at[tuple(spot)].set(low)
    longest = extent.index(max(extent))
    spot[longest] = (spot[longest] + 1) % extent[longest]
    return drawn.at[tuple(spot)].set(high)


def setup_inputs(seed: int = 0) -> dict:
    splits = jax.random.split(jax.random.key(seed), 4)
    return {
        "interface_rows": draw_interface_rows(jax.random.fold_in(splits[3], 71), 0),
        "exterior_rows": draw_exterior_rows(jax.random.fold_in(splits[3], 71), 0),
        "pml_mask": set_ends((jax.random.randint(splits[2], (SLOTS, BOXES, M), 0, 4) < 1).astype(jnp.int32), jax.random.fold_in(splits[2], 1), 0, 1),
    }


pml_damping = 2.0

def damped(rows, offset, mask_row):
    count = rows.shape[-2]
    width = rows.shape[-1]
    match_table = (jnp.arange(count)[:, None] + offset == jnp.arange(width)[None, :]).astype(jnp.float32)
    return rows + match_table * (pml_damping * mask_row.astype(jnp.float32))[..., None, :]

def cholesky_solve(factor, right):
    forward = lax.linalg.triangular_solve(factor, right, left_side=True, lower=True, transpose_a=False)
    return lax.linalg.triangular_solve(factor, forward, left_side=True, lower=True, transpose_a=True)

def solve_pair(upper_first, upper_second, inner):
    schur = upper_first[..., :inner] + upper_second[..., :inner]
    coupled = jnp.concatenate([upper_first[..., inner:], upper_second[..., inner:]], axis=-1)
    factor = jnp.linalg.cholesky(schur)
    return cholesky_solve(factor, coupled)

def place_and_correct(lower_rows, solved, place_first, inner):
    outer = lower_rows[..., inner:]
    blank = jnp.zeros_like(outer)
    placed = jnp.where(place_first, jnp.concatenate([outer, blank], axis=-1), jnp.concatenate([blank, outer], axis=-1))
    correction = jnp.einsum('...rk,...kc->...rc', lower_rows[..., :inner], solved, precision=lax.Precision.HIGHEST)
    return placed - correction

def reorder(rows, segment):
    width = rows.shape[-1]
    lead = rows.shape[:-1]
    grouped = rows.reshape(lead + (width // (2 * segment), 2, segment))
    shared = grouped[..., 0, :].reshape(lead + (width // 2,))
    others = grouped[..., 1, :].reshape(lead + (width // 2,))
    return jnp.concatenate([shared, others], axis=-1)

def reference(interface_rows, exterior_rows, pml_mask):
    inner_rows = damped(interface_rows, 0, pml_mask)
    outer_rows = damped(exterior_rows, K, pml_mask)
    paired_inner = inner_rows.reshape(SLOTS, BOXES // 2, 2, K, M)
    paired_outer = outer_rows.reshape(SLOTS, BOXES // 2, 2, R, M)
    solved = solve_pair(paired_inner[:, :, 0], paired_inner[:, :, 1], K)
    rows_first = place_and_correct(paired_outer[:, :, 0], solved, True, K)
    rows_second = place_and_correct(paired_outer[:, :, 1], solved, False, K)
    level_one = jnp.stack([rows_first, rows_second], axis=2).reshape(SLOTS, BOXES, R, 2 * R)
    merged = level_one.reshape(SLOTS, BOXES // 2, 2 * R, 2 * R)
    grouped = merged.reshape(SLOTS, BOXES // 2, R // SEGMENT, 2, SEGMENT, 2 * R)
    shared_rows = reorder(grouped[:, :, :, 0].reshape(SLOTS, BOXES // 2, R, 2 * R), SEGMENT)
    other_rows = reorder(grouped[:, :, :, 1].reshape(SLOTS, BOXES // 2, R, 2 * R), SEGMENT)
    paired_shared = shared_rows.reshape(SLOTS, BOXES // 4, 2, R, 2 * R)
    paired_others = other_rows.reshape(SLOTS, BOXES // 4, 2, R, 2 * R)
    solved_two = solve_pair(paired_shared[:, :, 0], paired_shared[:, :, 1], R)
    upper_two = place_and_correct(paired_others[:, :, 0], solved_two, True, R)
    lower_two = place_and_correct(paired_others[:, :, 1], solved_two, False, R)
    level_two = jnp.concatenate([upper_two, lower_two], axis=2).reshape(SLOTS, BOXES, R // 2, 2 * R)
    return (level_one, level_two)
```

```python
import functools

import jax
import jax.numpy as jnp
from jax import lax
from jax.experimental import pallas as pl
from jax.experimental.pallas import tpu as pltpu
from jax.sharding import Mesh
from jax.sharding import PartitionSpec as P

HI = lax.Precision.HIGHEST
DAMPING = 2.0
VMEM_LIMIT = 48 * 2**20
PLANE = ("xh", "xl", "z")


def dot(a, b):
    return jnp.dot(a, b, precision=HI, preferred_element_type=jnp.float32)


def dot_nt(a, b):
    return lax.dot_general(
        a, b, (((1,), (1,)), ((), ())), precision=HI, preferred_element_type=jnp.float32
    )


def small_sweep(entries):
    n = len(entries)
    a = [[entries[max(i, j)][min(i, j)] for j in range(n)] for i in range(n)]
    for k in range(n):
        r = 1.0 / a[k][k]
        u = [a[k][j] * r for j in range(n)]
        new = [[None] * n for _ in range(n)]
        for i in range(n):
            for j in range(i + 1):
                if i == k and j == k:
                    v = -r
                elif i == k:
                    v = u[j]
                elif j == k:
                    v = u[i]
                else:
                    v = a[i][j] - a[i][k] * u[j]
                new[i][j] = v
                new[j][i] = v
        a = new
    return a


def tree_sum(t):
    while len(t) > 1:
        t = [t[i] + t[i + 1] for i in range(0, len(t) - 1, 2)] + ([t[-1]] if len(t) % 2 else [])
    return t[0]


def pivot_rows(row, k, lane):
    w = row.shape[1]
    inblk = (lane >= 8 * k) & (lane < 8 * k + 8)
    col = [jnp.broadcast_to(row[:, 8 * k + q : 8 * k + q + 1], (8, w)) for q in range(8)]
    entries = [
        [jnp.broadcast_to(col[j][i : i + 1], (8, w)) if j <= i else None for j in range(8)]
        for i in range(8)
    ]
    m = small_sweep(entries)
    rb = [
        jnp.where(
            inblk,
            jnp.where(lane == 8 * k + j, -1.0, 0.0),
            jnp.broadcast_to(row[j : j + 1], (8, w)),
        )
        for j in range(8)
    ]
    return [tree_sum([m[i][j] * rb[j] for j in range(8)]) for i in range(8)]


def sweep_blocks(mats):
    n = 128
    steps = n // 8
    lane = lax.broadcasted_iota(jnp.int32, (8, n), 1)
    sub = lax.broadcasted_iota(jnp.int32, (8, n), 0)
    full_lane = lax.broadcasted_iota(jnp.int32, (n, n), 1)
    mats = list(mats)
    rows = [a[0:8] for a in mats]
    for k in range(steps):
        inblk = (lane >= 8 * k) & (lane < 8 * k + 8)
        full_in = (full_lane >= 8 * k) & (full_lane < 8 * k + 8)
        next_mats, next_rows = [], []
        for a, row in zip(mats, rows):
            news = pivot_rows(row, k, lane)
            packed = news[7]
            for i in range(7):
                packed = jnp.where(sub == i, news[i], packed)
            if k < steps - 1:
                ahead = a[8 * k + 8 : 8 * k + 16]
                terms = [
                    jnp.broadcast_to(ahead[:, 8 * k + q : 8 * k + q + 1], (8, n)) * news[q]
                    for q in range(8)
                ]
                next_rows.append(jnp.where(inblk, 0.0, ahead) + tree_sum(terms))
            zero = jnp.zeros((8, n), jnp.float32)
            spread = jnp.concatenate([packed if v == k else zero for v in range(steps)], 0)
            full = jnp.where(full_in, 0.0, a) + dot(jnp.where(full_in, a, 0.0), spread)
            parts = ([full[: 8 * k]] if k > 0 else []) + [-packed]
            if k < steps - 1:
                parts.append(next_rows[-1])
                if k < steps - 2:
                    parts.append(full[8 * k + 16 :])
            next_mats.append(jnp.concatenate(parts, 0))
        mats, rows = next_mats, next_rows
    return mats


def sweep_refs(refs, kb):
    at = pl.ds(pl.multiple_of(kb * 128, 128), 128)
    inverses = sweep_blocks([ref[at, at] for ref in refs])
    for ref, x in zip(refs, inverses):
        minus = dot(x, ref[at, :])
        column = ref[:, at]
        side = dot(column, x)
        ref[...] = ref[...] + dot(column, minus)
        ref[at, :] = -minus
        ref[:, at] = -side
        ref[at, at] = x


def lane_index(rows, back):
    lane = lax.broadcasted_iota(jnp.int32, (rows, 128), 1)
    if back:
        seg = lane // 16
        return (seg % 2) * 64 + (seg // 2) * 16 + lane % 16
    half = lane // 64
    return ((lane % 64) // 16) * 32 + half * 16 + lane % 16


def pick(x, index):
    return jnp.take_along_axis(x, index, axis=1)


def split_columns(x):
    rows = x.shape[0]
    index = lane_index(rows, False)
    low = lax.broadcasted_iota(jnp.int32, (rows, 128), 1) < 64
    shared, other = [], []
    for j in range(3):
        a = pick(x[:, 256 * j : 256 * j + 128], index)
        b = pick(x[:, 256 * j + 128 : 256 * j + 256], index)
        shared.append(jnp.where(low, a, pltpu.roll(b, 64, 1)))
        other.append(jnp.where(low, pltpu.roll(a, 64, 1), b))
    return shared + other


def join_columns(panels):
    rows = panels[0].shape[0]
    index = lane_index(rows, True)
    low = lax.broadcasted_iota(jnp.int32, (rows, 128), 1) < 64
    out = []
    for j in range(3):
        s, o = panels[j], panels[3 + j]
        out.append(pick(jnp.where(low, s, pltpu.roll(o, 64, 1)), index))
        out.append(pick(jnp.where(low, pltpu.roll(s, 64, 1), o), index))
    return out


def shared_rows(x):
    return jnp.concatenate([x[0:16], x[32:48], x[64:80]], 0)


def other_rows(x):
    return jnp.concatenate([x[16:32], x[48:64], x[80:96]], 0)


def choose(first, a, b):
    return jnp.where(first, a, b), jnp.where(first, b, a)


def damp_kernel(where_ref, inner_ref, outer_ref, mask_ref, mine_ref, send_ref):
    core, blk = where_ref[0], where_ref[1]
    for out_ref, slot in ((mine_ref, core), (send_ref, 1 - core)):
        gain = DAMPING * mask_ref[slot].astype(jnp.float32)
        for source, start, count, offset in (
            (inner_ref, 0, 32, blk * 32),
            (outer_ref, 32, 96, 256 + blk * 96),
        ):
            row = lax.broadcasted_iota(jnp.int32, (count, 1024), 0) + offset
            lane = lax.broadcasted_iota(jnp.int32, (count, 1024), 1)
            match = jnp.where(row == lane, 1.0, 0.0)
            out_ref[start : start + count, :] = source[slot] + match * gain


def split_kernel(
    where_ref, mine_ref, recv_ref, keep_ref, send_ref, s1_ref, bulk_ref, es_ref, ei_ref, lee_ref
):
    first = where_ref[0] == 0
    upper = where_ref[2] == 0
    boxes = choose(first, mine_ref[...], recv_ref[...])
    total = boxes[0][0:32, 0:256] + boxes[1][0:32, 0:256]
    s1_ref[0] = total[:, 0:128]
    s1_ref[1] = total[:, 128:256]
    kept = []
    for t, box in enumerate(boxes):
        panels = split_columns(box[:, 256:1024])
        for j in range(6):
            bulk_ref[32 * (6 * t + j) : 32 * (6 * t + j) + 32, :] = panels[j][0:32]
        for j in range(3):
            base = 384 + 144 * t + 48 * j
            bulk_ref[base : base + 48, :] = shared_rows(panels[3 + j][32:128])
            es_ref[t, :, 128 * j : 128 * j + 128] = other_rows(panels[j][32:128])
            lee_ref[t, :, 128 * j : 128 * j + 128] = other_rows(panels[3 + j][32:128])
        ei_ref[t] = other_rows(box[32:128, 0:256])
        kept.append([shared_rows(panels[j][32:128]) for j in range(3)])
    for j in range(3):
        keep_ref[j], send_ref[j] = choose(upper, kept[0][j], kept[1][j])


def first_kernel(where_ref, early_ref, d_ref, s_ref, a_ref, b_ref, c_ref):
    pair = where_ref[2]
    row = lax.broadcasted_iota(jnp.int32, (384, 384), 0)
    lane = lax.broadcasted_iota(jnp.int32, (384, 384), 1)
    c_ref[...] = jnp.where(row == lane, 1.0, 0.0)
    for k in range(8):
        for j in range(3):
            at = (slice(48 * k, 48 * k + 48), slice(128 * j, 128 * j + 128))
            a_ref[at] = early_ref[k, 48 * j : 48 * j + 48]
            b_ref[at] = early_ref[8 + k, 48 * j : 48 * j + 48]
        for j in range(2):
            c_ref[32 * k : 32 * k + 32, 128 * j : 128 * j + 128] = early_ref[
                8 * pair + k, 144 + 32 * j : 176 + 32 * j
            ]

    def step(kb, carry):
        sweep_refs([a_ref, b_ref, c_ref], kb)
        return carry

    lax.fori_loop(0, 3, step, 0)
    d_ref[0] = -a_ref[...]
    d_ref[1] = -b_ref[...]
    s_ref[...] = -c_ref[0:256, 0:256]


def one_kernel(where_ref, bulk_ref, s_ref, mine_ref, recv_ref, keep_ref, send_ref, u_ref):
    first = where_ref[0] == 0
    pair = where_ref[2]
    for k in range(8):
        for j in range(12):
            u_ref[32 * k : 32 * k + 32, 128 * j : 128 * j + 128] = bulk_ref[
                8 * pair + k, 32 * j : 32 * j + 32
            ]
    boxes = choose(first, mine_ref[32:128, :], recv_ref[32:128, :])
    left = jnp.concatenate([boxes[0][:, 0:256], boxes[1][:, 0:256]], 0)
    right = dot(dot(left, s_ref[...]), u_ref[...])
    outs = []
    for t in range(2):
        block = right[96 * t : 96 * t + 96]
        panels = []
        for h in range(2):
            part = join_columns(
                [block[:, 768 * h + 128 * j : 768 * h + 128 * j + 128] for j in range(6)]
            )
            for j in range(6):
                if h == t:
                    panels.append(boxes[t][:, 256 + 128 * j : 384 + 128 * j] - part[j])
                else:
                    panels.append(-part[j])
        outs.append(jnp.concatenate(panels, 1))
    keep_ref[...], send_ref[...] = choose(first, outs[0], outs[1])


def two_kernel(
    where_ref,
    bulk_ref,
    early_ref,
    d_ref,
    es_ref,
    ei_ref,
    lee_ref,
    keep_ref,
    send_ref,
    u_ref,
    v_ref,
    c_ref,
    l_ref,
):
    first = where_ref[0] == 0
    upper = where_ref[2] == 0
    for p in range(2):
        for k in range(8):
            at = slice(256 * p + 32 * k, 256 * p + 32 * k + 32)
            for t in range(2):
                for j in range(3):
                    base = 32 * (6 * t + j)
                    u_ref[at, 384 * t + 128 * j : 384 * t + 128 * j + 128] = bulk_ref[
                        8 * p + k, base : base + 32
                    ]
    for t in range(2):
        v_ref[:, 384 * t : 384 * t + 384] = dot(u_ref[:, 384 * t : 384 * t + 384], d_ref[t])
    c_ref[...] = -dot_nt(v_ref[...], u_ref[...])
    for p in range(2):
        for k in range(8):
            for j in range(2):
                at = (
                    slice(256 * p + 32 * k, 256 * p + 32 * k + 32),
                    slice(256 * p + 128 * j, 256 * p + 128 * j + 128),
                )
                c_ref[at] = c_ref[at] + early_ref[8 * p + k, 144 + 32 * j : 176 + 32 * j]

    def step(kb, carry):
        sweep_refs([c_ref], kb)
        return carry

    lax.fori_loop(0, 4, step, 0)
    blank = jnp.zeros((48, 256), jnp.float32)
    rows, direct = [], []
    for t in range(2):
        low, high = choose(upper, ei_ref[t], blank)
        placed = jnp.concatenate([low, high], 1)
        rows.append(placed - dot_nt(es_ref[t], v_ref[:, 384 * t : 384 * t + 384]))
        direct.append(dot(es_ref[t], d_ref[t]))
    none = jnp.zeros((48, 384), jnp.float32)
    g = -dot(jnp.concatenate(rows, 0), c_ref[...])
    t_s = (
        jnp.concatenate(
            [
                jnp.concatenate([direct[0], none], 1),
                jnp.concatenate([none, direct[1]], 1),
            ],
            0,
        )
        - dot(g, v_ref[...])
    )
    columns = []
    for p in range(2):
        for t in range(2):
            for k in range(8):
                for j in range(3):
                    base = 384 + 144 * t + 48 * j
                    l_ref[48 * k : 48 * k + 48, 128 * j : 128 * j + 128] = bulk_ref[
                        8 * p + k, base : base + 48
                    ]
                    base = 32 * (6 * t + 3 + j)
                    l_ref[384 + 32 * k : 416 + 32 * k, 128 * j : 128 * j + 128] = bulk_ref[
                        8 * p + k, base : base + 32
                    ]
            weights = jnp.concatenate(
                [t_s[:, 384 * t : 384 * t + 384], g[:, 256 * p : 256 * p + 256]], 1
            )
            own = jnp.where(where_ref[2] == p, lee_ref[t], 0.0)
            placed = jnp.concatenate([own, none] if t == 0 else [none, own], 0)
            columns.append(placed - dot(weights, l_ref[...]))
    out = jnp.concatenate(columns, 1)
    keep_ref[...], send_ref[...] = choose(first, out[0:48], out[48:96])


def call(kernel, outs, args, scratch=()):
    shapes = [jax.ShapeDtypeStruct(s, jnp.float32) for s in outs]
    specs = [pl.BlockSpec(memory_space=pltpu.SMEM)]
    specs += [pl.BlockSpec(memory_space=pltpu.VMEM) for _ in args[1:]]
    return pl.pallas_call(
        kernel,
        out_shape=shapes,
        in_specs=specs,
        out_specs=[pl.BlockSpec(memory_space=pltpu.VMEM) for _ in outs],
        scratch_shapes=[pltpu.VMEM(s, jnp.float32) for s in scratch],
        compiler_params=pltpu.CompilerParams(vmem_limit_bytes=VMEM_LIMIT),
    )(*args)


def swap(x, axis):
    return lax.ppermute(x, axis, [(0, 1), (1, 0)])


def by_slot(core, mine, other):
    first = core == 0
    return jnp.stack([jnp.where(first, mine, other), jnp.where(first, other, mine)])[:, None]


def local(interface_rows, exterior_rows, pml_mask):
    core = lax.axis_index("core")
    blk = lax.axis_index(("xl", "z"))
    where = jnp.stack([core, blk, lax.axis_index("xh")]).astype(jnp.int32)
    mine, send = call(
        damp_kernel,
        [(128, 1024), (128, 1024)],
        [where, interface_rows[:, 0], exterior_rows[:, 0], pml_mask],
    )
    recv = swap(send, "core")
    keep, away, s1, bulk, es, ei, lee = call(
        split_kernel,
        [
            (3, 48, 128),
            (3, 48, 128),
            (2, 32, 128),
            (672, 128),
            (2, 48, 384),
            (2, 48, 256),
            (2, 48, 384),
        ],
        [where, mine, recv],
    )
    bulk_all = lax.all_gather(bulk, PLANE, axis=0, tiled=False)
    shared = keep + swap(away, "xh")
    early = jnp.concatenate([shared.reshape(144, 128), s1.reshape(64, 128)], 0)
    early_all = lax.all_to_all(
        jnp.broadcast_to(early[None], (16, 208, 128)), PLANE, 0, 0, tiled=False
    )
    d_inv, s_inv = call(
        first_kernel,
        [(2, 384, 384), (256, 256)],
        [where, early_all],
        scratch=[(384, 384)] * 3,
    )
    one_keep, one_send = call(
        one_kernel,
        [(96, 1536), (96, 1536)],
        [where, bulk_all, s_inv, mine, recv],
        scratch=[(256, 1536)],
    )
    one_recv = swap(one_send, "core")
    two_keep, two_send = call(
        two_kernel,
        [(48, 1536), (48, 1536)],
        [where, bulk_all, early_all, d_inv, es, ei, lee],
        scratch=[(512, 768), (512, 768), (512, 512), (640, 384)],
    )
    two_recv = swap(two_send, "core")
    return by_slot(core, one_keep, one_recv), by_slot(core, two_keep, two_recv)


def solution(mesh):
    fine = Mesh(mesh.devices.reshape(4, 2, 2, 2, 4), ("y", "xh", "core", "xl", "z"))
    box, blk = ("y", "xh", "core"), ("xl", "z")
    rows = P(None, box, blk, None)
    return jax.shard_map(
        local,
        mesh=fine,
        in_specs=(rows, rows, P(None, box, None)),
        out_specs=(rows, rows),
        check_vma=False,
    )
```

```python
import functools

import jax
import jax.numpy as jnp
from jax import lax
from jax.experimental import pallas as pl
from jax.experimental.pallas import tpu as pltpu
from jax.sharding import Mesh
from jax.sharding import PartitionSpec as P

HI = lax.Precision.HIGHEST
DAMPING = 2.0
PLANE = ("xh", "xl", "z")


def dot(a, b):
    return jnp.dot(a, b, precision=HI, preferred_element_type=jnp.float32)


def dot_nt(a, b):
    return lax.dot_general(
        a, b, (((1,), (1,)), ((), ())), precision=HI, preferred_element_type=jnp.float32
    )


PANEL = 16


def tree_sum(t):
    while len(t) > 1:
        t = [t[i] + t[i + 1] for i in range(0, len(t) - 1, 2)] + ([t[-1]] if len(t) % 2 else [])
    return t[0]


def spread_lane(x, at):
    return jnp.broadcast_to(x[:, at : at + 1], x.shape)


def spread_row(x, at):
    return jnp.broadcast_to(x[at : at + 1], x.shape)


def eliminate(rows, base, lane, sub):
    count = 8 * len(rows)
    cols = [[spread_lane(x, base + q) for x in rows] for q in range(count)]
    inblk = (lane >= base) & (lane < base + count)
    out = [
        jnp.where(inblk, jnp.where(lane == sub + (8 * v + base), -1.0, 0.0), x)
        for v, x in enumerate(rows)
    ]
    for k in range(count):
        kv, ks = divmod(k, 8)
        scale = 1.0 / spread_row(cols[k][kv], ks)
        hit = sub == ks

        def update(tiles):
            row = spread_row(tiles[kv], ks) * scale
            new = [x - c * row for x, c in zip(tiles, cols[k])]
            new[kv] = jnp.where(hit, row, new[kv])
            return new

        for j in range(k + 1, count):
            cols[j] = update(cols[j])
        out = update(out)
    return out


def sweep_blocks(mats):
    tiles, per = 16, PANEL // 8
    lane = lax.broadcasted_iota(jnp.int32, (8, 128), 1)
    sub = lax.broadcasted_iota(jnp.int32, (8, 128), 0)
    mats = [[a[8 * i : 8 * i + 8] for i in range(tiles)] for a in mats]
    for k in range(tiles // per):
        base = PANEL * k
        inblk = (lane >= base) & (lane < base + PANEL)
        own = range(per * k, per * k + per)
        near = range(per * k + per, min(per * k + 2 * per, tiles))
        for c, rows in enumerate(mats):
            cols = {t: [spread_lane(rows[t], base + q) for q in range(PANEL)] for t in near}
            solved = eliminate([rows[t] for t in own], base, lane, sub)
            new = list(rows)
            if near:
                each = [spread_row(solved[q // 8], q % 8) for q in range(PANEL)]
                for t in near:
                    total = tree_sum([cols[t][q] * each[q] for q in range(PANEL)])
                    new[t] = jnp.where(inblk, 0.0, rows[t]) - total
            change = lax.dot_general(
                jnp.concatenate([rows[t] for t in own], 0),
                jnp.concatenate(solved, 0),
                (((0,), (0,)), ((), ())),
                precision=HI,
                preferred_element_type=jnp.float32,
            )
            for t in range(tiles):
                if t in own:
                    new[t] = solved[t - per * k]
                elif t not in near:
                    new[t] = jnp.where(inblk, 0.0, rows[t]) - change[8 * t : 8 * t + 8]
            mats[c] = new
    return [jnp.concatenate(rows, 0) for rows in mats]


def sweep_refs(refs, kb):
    at = pl.ds(pl.multiple_of(kb * 128, 128), 128)
    inverses = sweep_blocks([ref[at, at] for ref in refs])
    for ref, x in zip(refs, inverses):
        minus = dot(x, ref[at, :])
        column = ref[:, at]
        side = dot(column, x)
        ref[...] = ref[...] + dot(column, minus)
        ref[at, :] = -minus
        ref[:, at] = -side
        ref[at, at] = x


def lane_index(rows, back):
    lane = lax.broadcasted_iota(jnp.int32, (rows, 128), 1)
    if back:
        seg = lane // 16
        return (seg % 2) * 64 + (seg // 2) * 16 + lane % 16
    half = lane // 64
    return ((lane % 64) // 16) * 32 + half * 16 + lane % 16


def pick(x, index):
    return jnp.take_along_axis(x, index, axis=1)


def split_columns(x):
    rows = x.shape[0]
    index = lane_index(rows, False)
    low = lax.broadcasted_iota(jnp.int32, (rows, 128), 1) < 64
    shared, other = [], []
    for j in range(3):
        a = pick(x[:, 256 * j : 256 * j + 128], index)
        b = pick(x[:, 256 * j + 128 : 256 * j + 256], index)
        shared.append(jnp.where(low, a, pltpu.roll(b, 64, 1)))
        other.append(jnp.where(low, pltpu.roll(a, 64, 1), b))
    return shared + other


def join_columns(panels):
    rows = panels[0].shape[0]
    index = lane_index(rows, True)
    low = lax.broadcasted_iota(jnp.int32, (rows, 128), 1) < 64
    out = []
    for j in range(3):
        s, o = panels[j], panels[3 + j]
        out.append(pick(jnp.where(low, s, pltpu.roll(o, 64, 1)), index))
        out.append(pick(jnp.where(low, pltpu.roll(s, 64, 1), o), index))
    return out


def shared_rows(x):
    return jnp.concatenate([x[0:16], x[32:48], x[64:80]], 0)


def other_rows(x):
    return jnp.concatenate([x[16:32], x[48:64], x[80:96]], 0)


def choose(first, a, b):
    return jnp.where(first, a, b), jnp.where(first, b, a)


def damp_kernel(
    where_ref, inner_hbm, outer_hbm, mask_hbm, mine_ref, send_ref, inner_ref, outer_ref, mask_ref, sems
):
    copies = [
        pltpu.make_async_copy(a, b, sems.at[i])
        for i, (a, b) in enumerate(
            ((mask_hbm, mask_ref), (inner_hbm, inner_ref), (outer_hbm, outer_ref))
        )
    ]
    for copy in copies:
        copy.start()
    for copy in copies:
        copy.wait()
    core, blk = where_ref[0], where_ref[1]
    for out_ref, slot in ((mine_ref, core), (send_ref, 1 - core)):
        gain = DAMPING * mask_ref[slot, 0].astype(jnp.float32)
        for source, start, count, offset in (
            (inner_ref, 0, 32, blk * 32),
            (outer_ref, 32, 96, 256 + blk * 96),
        ):
            row = lax.broadcasted_iota(jnp.int32, (count, 1024), 0) + offset
            lane = lax.broadcasted_iota(jnp.int32, (count, 1024), 1)
            match = jnp.where(row == lane, 1.0, 0.0)
            out_ref[start : start + count, :] = source[slot, 0] + match * gain


def split_kernel(
    where_ref, mine_ref, recv_ref, keep_ref, send_ref, s1_ref, bulk_ref, es_ref, ei_ref, lee_ref
):
    first = where_ref[0] == 0
    upper = where_ref[2] == 0
    boxes = choose(first, mine_ref[...], recv_ref[...])
    total = boxes[0][0:32, 0:256] + boxes[1][0:32, 0:256]
    s1_ref[0] = total[:, 0:128]
    s1_ref[1] = total[:, 128:256]
    kept = []
    for t, box in enumerate(boxes):
        panels = split_columns(box[:, 256:1024])
        for j in range(6):
            bulk_ref[32 * (6 * t + j) : 32 * (6 * t + j) + 32, :] = panels[j][0:32]
        for j in range(3):
            base = 384 + 144 * t + 48 * j
            bulk_ref[base : base + 48, :] = shared_rows(panels[3 + j][32:128])
            es_ref[t, :, 128 * j : 128 * j + 128] = other_rows(panels[j][32:128])
            lee_ref[t, :, 128 * j : 128 * j + 128] = other_rows(panels[3 + j][32:128])
        ei_ref[t] = other_rows(box[32:128, 0:256])
        kept.append([shared_rows(panels[j][32:128]) for j in range(3)])
    for j in range(3):
        keep_ref[j], send_ref[j] = choose(upper, kept[0][j], kept[1][j])


def first_kernel(early_ref, d_ref):
    for k in range(8):
        for j in range(3):
            at = (slice(48 * k, 48 * k + 48), slice(128 * j, 128 * j + 128))
            for t in range(2):
                d_ref[(t,) + at] = early_ref[8 * t + k, 48 * j : 48 * j + 48]

    def step(kb, carry):
        sweep_refs([d_ref.at[0], d_ref.at[1]], kb)
        return carry

    lax.fori_loop(0, 3, step, 0)
    d_ref[...] = -d_ref[...]


def inner_kernel(s1_ref, out_ref):
    for k in range(8):
        for j in range(2):
            out_ref[32 * k : 32 * k + 32, 128 * j : 128 * j + 128] = s1_ref[k, j]

    def step(kb, carry):
        sweep_refs([out_ref], kb)
        return carry

    lax.fori_loop(0, 2, step, 0)
    out_ref[...] = -out_ref[...]


def one_kernel(
    where_ref, bulk_hbm, s_ref, mine_ref, recv_ref, keep_ref, send_ref, bulk_ref, u_ref, sems
):
    first = where_ref[0] == 0
    pair = where_ref[2]
    copies = [
        pltpu.make_async_copy(bulk_hbm.at[8 * pair + k, 0:384], bulk_ref.at[k], sems.at[k])
        for k in range(8)
    ]
    for copy in copies:
        copy.start()
    boxes = choose(first, mine_ref[32:128, :], recv_ref[32:128, :])
    left = jnp.concatenate([boxes[0][:, 0:256], boxes[1][:, 0:256]], 0)
    left = dot(left, s_ref[...])
    for k, copy in enumerate(copies):
        copy.wait()
        for j in range(12):
            u_ref[32 * k : 32 * k + 32, 128 * j : 128 * j + 128] = bulk_ref[
                k, 32 * j : 32 * j + 32
            ]
    right = dot(left, u_ref[...])
    outs = []
    for t in range(2):
        block = right[96 * t : 96 * t + 96]
        panels = []
        for h in range(2):
            part = join_columns(
                [block[:, 768 * h + 128 * j : 768 * h + 128 * j + 128] for j in range(6)]
            )
            for j in range(6):
                if h == t:
                    panels.append(boxes[t][:, 256 + 128 * j : 384 + 128 * j] - part[j])
                else:
                    panels.append(-part[j])
        outs.append(jnp.concatenate(panels, 1))
    keep_ref[...], send_ref[...] = choose(first, outs[0], outs[1])


def two_kernel(
    where_ref,
    bulk_hbm,
    s1_ref,
    s1_far_ref,
    d_ref,
    es_ref,
    ei_ref,
    lee_ref,
    keep_ref,
    send_ref,
    u_ref,
    v_ref,
    c_ref,
    l_ref,
    bulk_ref,
    sems,
):
    first = where_ref[0] == 0
    upper = where_ref[2] == 0
    parts = (slice(0, 384), slice(384, 672))
    copies = [
        [
            pltpu.make_async_copy(
                bulk_hbm.at[i, part], bulk_ref.at[i, part], sems.at[16 * h + i]
            )
            for i in range(16)
        ]
        for h, part in enumerate(parts)
    ]
    for group in copies:
        for copy in group:
            copy.start()
    for copy in copies[0]:
        copy.wait()
    for p in range(2):
        for k in range(8):
            at = slice(256 * p + 32 * k, 256 * p + 32 * k + 32)
            for t in range(2):
                for j in range(3):
                    base = 32 * (6 * t + j)
                    u_ref[at, 384 * t + 128 * j : 384 * t + 128 * j + 128] = bulk_ref[
                        8 * p + k, base : base + 32
                    ]
    for t in range(2):
        v_ref[:, 384 * t : 384 * t + 384] = dot(u_ref[:, 384 * t : 384 * t + 384], d_ref[t])
    c_ref[...] = -dot_nt(v_ref[...], u_ref[...])
    for k in range(8):
        for j in range(2):
            for p, block in enumerate(choose(upper, s1_ref[k, j], s1_far_ref[k, j])):
                at = (
                    slice(256 * p + 32 * k, 256 * p + 32 * k + 32),
                    slice(256 * p + 128 * j, 256 * p + 128 * j + 128),
                )
                c_ref[at] = c_ref[at] + block

    def step(kb, carry):
        sweep_refs([c_ref], kb)
        return carry

    lax.fori_loop(0, 4, step, 0)
    blank = jnp.zeros((48, 256), jnp.float32)
    rows, direct = [], []
    for t in range(2):
        low, high = choose(upper, ei_ref[t], blank)
        placed = jnp.concatenate([low, high], 1)
        rows.append(placed - dot_nt(es_ref[t], v_ref[:, 384 * t : 384 * t + 384]))
        direct.append(dot(es_ref[t], d_ref[t]))
    none = jnp.zeros((48, 384), jnp.float32)
    g = -dot(jnp.concatenate(rows, 0), c_ref[...])
    t_s = (
        jnp.concatenate(
            [
                jnp.concatenate([direct[0], none], 1),
                jnp.concatenate([none, direct[1]], 1),
            ],
            0,
        )
        - dot(g, v_ref[...])
    )
    for copy in copies[1]:
        copy.wait()
    columns = []
    for p in range(2):
        for t in range(2):
            for k in range(8):
                for j in range(3):
                    base = 384 + 144 * t + 48 * j
                    l_ref[48 * k : 48 * k + 48, 128 * j : 128 * j + 128] = bulk_ref[
                        8 * p + k, base : base + 48
                    ]
                    base = 32 * (6 * t + 3 + j)
                    l_ref[384 + 32 * k : 416 + 32 * k, 128 * j : 128 * j + 128] = bulk_ref[
                        8 * p + k, base : base + 32
                    ]
            weights = jnp.concatenate(
                [t_s[:, 384 * t : 384 * t + 384], g[:, 256 * p : 256 * p + 256]], 1
            )
            own = jnp.where(where_ref[2] == p, lee_ref[t], 0.0)
            placed = jnp.concatenate([own, none] if t == 0 else [none, own], 0)
            columns.append(placed - dot(weights, l_ref[...]))
    out = jnp.concatenate(columns, 1)
    keep_ref[...], send_ref[...] = choose(first, out[0:48], out[48:96])


def call(kernel, outs, args, micros, limit, scratch=(), scalars=True, hbm=0):
    shapes = [jax.ShapeDtypeStruct(s, jnp.float32) for s in outs]
    specs = [pl.BlockSpec(memory_space=pltpu.SMEM)] if scalars else []
    specs += [pl.BlockSpec(memory_space=pltpu.HBM)] * hbm
    specs += [pl.BlockSpec(memory_space=pltpu.VMEM)] * (len(args) - len(specs))
    return pl.pallas_call(
        kernel,
        out_shape=shapes,
        in_specs=specs,
        out_specs=[pl.BlockSpec(memory_space=pltpu.VMEM) for _ in outs],
        scratch_shapes=scratch,
        compiler_params=pltpu.CompilerParams(vmem_limit_bytes=limit * 2**20),
        cost_estimate=pl.CostEstimate(
            flops=int(micros * 1e9), bytes_accessed=2**20, transcendentals=0
        ),
    )(*args)


def swap(x, axis):
    return lax.ppermute(x, axis, [(0, 1), (1, 0)])


def ring_gather(x):
    z = lax.axis_index("z")
    parts = [x] + [lax.ppermute(x, "z", [(i, (i + d) % 4) for i in range(4)]) for d in (1, 2, 3)]
    ordered = []
    for owner in range(4):
        step = (z - owner) % 4
        ordered.append(
            jnp.where(
                step < 2,
                jnp.where(step == 0, parts[0], parts[1]),
                jnp.where(step == 2, parts[2], parts[3]),
            )
        )
    return jnp.stack(ordered)


def by_slot(core, mine, other):
    first = core == 0
    return jnp.stack([jnp.where(first, mine, other), jnp.where(first, other, mine)])[:, None]


def floats(*shape):
    return pltpu.VMEM(shape, jnp.float32)


def local(interface_rows, exterior_rows, pml_mask):
    core = lax.axis_index("core")
    blk = lax.axis_index(("xl", "z"))
    where = jnp.stack([core, blk, lax.axis_index("xh")]).astype(jnp.int32)
    mine, send = call(
        damp_kernel,
        [(128, 1024), (128, 1024)],
        [where, interface_rows, exterior_rows, pml_mask],
        1,
        8,
        hbm=3,
        scratch=[
            floats(2, 1, 32, 1024),
            floats(2, 1, 96, 1024),
            pltpu.VMEM((2, 1, 1024), jnp.int32),
            pltpu.SemaphoreType.DMA((3,)),
        ],
    )
    recv = swap(send, "core")
    keep, away, s1, bulk, es, ei, lee = call(
        split_kernel,
        [
            (3, 48, 128),
            (3, 48, 128),
            (2, 32, 128),
            (672, 128),
            (2, 48, 384),
            (2, 48, 256),
            (2, 48, 384),
        ],
        [where, mine, recv],
        2,
        8,
    )
    bulk_all = lax.all_gather(bulk, PLANE, axis=0, tiled=False)
    shared = keep + swap(away, "xh")
    near = ring_gather(s1)
    early_all = lax.all_to_all(
        jnp.broadcast_to(shared.reshape(144, 128), (16, 144, 128)), PLANE, 0, 0, tiled=False
    )
    near, early_all = lax.optimization_barrier((near, early_all))
    across = swap(near, "xl")
    (d_inv,) = call(first_kernel, [(2, 384, 384)], [early_all], 17, 12, scalars=False)
    low = lax.axis_index("xl") == 0
    s1_own = jnp.concatenate(
        [jnp.where(low, near, across), jnp.where(low, across, near)], 0
    )
    s1_own, d_inv = lax.optimization_barrier((s1_own, d_inv))
    s1_far = swap(s1_own, "xh")
    (s_inv,) = call(inner_kernel, [(256, 256)], [s1_own], 8, 8, scalars=False)
    one_keep, one_send = call(
        one_kernel,
        [(96, 1536), (96, 1536)],
        [where, bulk_all, s_inv, mine, recv],
        3,
        12,
        hbm=1,
        scratch=[floats(8, 384, 128), floats(256, 1536), pltpu.SemaphoreType.DMA((8,))],
    )
    one_recv = swap(one_send, "core")
    bulk_late, one_keep = lax.optimization_barrier((bulk_all, one_keep))
    two_keep, two_send = call(
        two_kernel,
        [(48, 1536), (48, 1536)],
        [where, bulk_late, s1_own, s1_far, d_inv, es, ei, lee],
        25,
        24,
        hbm=1,
        scratch=[
            floats(512, 768),
            floats(512, 768),
            floats(512, 512),
            floats(640, 384),
            floats(16, 672, 128),
            pltpu.SemaphoreType.DMA((32,)),
        ],
    )
    two_recv = swap(two_send, "core")
    return by_slot(core, one_keep, one_recv), by_slot(core, two_keep, two_recv)


def solution(mesh):
    fine = Mesh(mesh.devices.reshape(4, 2, 2, 2, 4), ("y", "xh", "core", "xl", "z"))
    box, blk = ("y", "xh", "core"), ("xl", "z")
    rows = P(None, box, blk, None)
    return jax.shard_map(
        local,
        mesh=fine,
        in_specs=(rows, rows, P(None, box, None)),
        out_specs=(rows, rows),
        check_vma=False,
    )
```

```python
import functools

import jax
import jax.numpy as jnp
from jax import lax
from jax.experimental import pallas as pl
from jax.experimental.pallas import tpu as pltpu
from jax.sharding import Mesh
from jax.sharding import PartitionSpec as P

HI = lax.Precision.HIGHEST
DAMPING = 2.0
PLANE = ("xh", "xl", "z")


def dot(a, b):
    return jnp.dot(a, b, precision=HI, preferred_element_type=jnp.float32)


def dot_nt(a, b):
    return lax.dot_general(
        a, b, (((1,), (1,)), ((), ())), precision=HI, preferred_element_type=jnp.float32
    )


PANEL = 16


def tree_sum(t):
    while len(t) > 1:
        t = [t[i] + t[i + 1] for i in range(0, len(t) - 1, 2)] + ([t[-1]] if len(t) % 2 else [])
    return t[0]


def spread_lane(x, at):
    return jnp.broadcast_to(x[:, at : at + 1], x.shape)


def spread_row(x, at):
    return jnp.broadcast_to(x[at : at + 1], x.shape)


def eliminate(rows, base, lane, sub):
    count = 8 * len(rows)
    cols = [[spread_lane(x, base + q) for x in rows] for q in range(count)]
    inblk = (lane >= base) & (lane < base + count)
    out = [
        jnp.where(inblk, jnp.where(lane == sub + (8 * v + base), -1.0, 0.0), x)
        for v, x in enumerate(rows)
    ]
    for k in range(count):
        kv, ks = divmod(k, 8)
        scale = 1.0 / spread_row(cols[k][kv], ks)
        hit = sub == ks

        def update(tiles):
            row = spread_row(tiles[kv], ks) * scale
            new = [x - c * row for x, c in zip(tiles, cols[k])]
            new[kv] = jnp.where(hit, row, new[kv])
            return new

        for j in range(k + 1, count):
            cols[j] = update(cols[j])
        out = update(out)
    return out


def sweep_blocks(mats, work=()):
    work = list(work)
    tiles, per = 16, PANEL // 8
    lane = lax.broadcasted_iota(jnp.int32, (8, 128), 1)
    sub = lax.broadcasted_iota(jnp.int32, (8, 128), 0)
    mats = [[a[8 * i : 8 * i + 8] for i in range(tiles)] for a in mats]
    for k in range(tiles // per):
        base = PANEL * k
        inblk = (lane >= base) & (lane < base + PANEL)
        own = range(per * k, per * k + per)
        near = range(per * k + per, min(per * k + 2 * per, tiles))
        for c, rows in enumerate(mats):
            cols = {t: [spread_lane(rows[t], base + q) for q in range(PANEL)] for t in near}
            solved = eliminate([rows[t] for t in own], base, lane, sub)
            new = list(rows)
            if near:
                each = [spread_row(solved[q // 8], q % 8) for q in range(PANEL)]
                for t in near:
                    total = tree_sum([cols[t][q] * each[q] for q in range(PANEL)])
                    new[t] = jnp.where(inblk, 0.0, rows[t]) - total
            change = lax.dot_general(
                jnp.concatenate([rows[t] for t in own], 0),
                jnp.concatenate(solved, 0),
                (((0,), (0,)), ((), ())),
                precision=HI,
                preferred_element_type=jnp.float32,
            )
            for t in range(tiles):
                if t in own:
                    new[t] = solved[t - per * k]
                elif t not in near:
                    new[t] = jnp.where(inblk, 0.0, rows[t]) - change[8 * t : 8 * t + 8]
            mats[c] = new
        left = tiles // per - k
        for _ in range(-(-len(work) // left)):
            work.pop(0)()
    return [jnp.concatenate(rows, 0) for rows in mats]


def sweep_refs(refs, kb):
    at = pl.ds(pl.multiple_of(kb * 128, 128), 128)
    inverses = sweep_blocks([ref[at, at] for ref in refs])
    for ref, x in zip(refs, inverses):
        minus = dot(x, ref[at, :])
        column = ref[:, at]
        side = dot(column, x)
        ref[...] = ref[...] + dot(column, minus)
        ref[at, :] = -minus
        ref[:, at] = -side
        ref[at, at] = x


def lane_index(rows, back):
    lane = lax.broadcasted_iota(jnp.int32, (rows, 128), 1)
    if back:
        seg = lane // 16
        return (seg % 2) * 64 + (seg // 2) * 16 + lane % 16
    half = lane // 64
    return ((lane % 64) // 16) * 32 + half * 16 + lane % 16


def pick(x, index):
    return jnp.take_along_axis(x, index, axis=1)


def split_columns(x):
    rows = x.shape[0]
    index = lane_index(rows, False)
    low = lax.broadcasted_iota(jnp.int32, (rows, 128), 1) < 64
    shared, other = [], []
    for j in range(3):
        a = pick(x[:, 256 * j : 256 * j + 128], index)
        b = pick(x[:, 256 * j + 128 : 256 * j + 256], index)
        shared.append(jnp.where(low, a, pltpu.roll(b, 64, 1)))
        other.append(jnp.where(low, pltpu.roll(a, 64, 1), b))
    return shared + other


def join_pair(shared, other):
    rows = shared.shape[0]
    index = lane_index(rows, True)
    low = lax.broadcasted_iota(jnp.int32, (rows, 128), 1) < 64
    return (
        pick(jnp.where(low, shared, pltpu.roll(other, 64, 1)), index),
        pick(jnp.where(low, pltpu.roll(shared, 64, 1), other), index),
    )


def shared_rows(x):
    return jnp.concatenate([x[0:16], x[32:48], x[64:80]], 0)


def other_rows(x):
    return jnp.concatenate([x[16:32], x[48:64], x[80:96]], 0)


def choose(first, a, b):
    return jnp.where(first, a, b), jnp.where(first, b, a)


def damp_kernel(
    where_ref, inner_hbm, outer_hbm, mask_hbm, mine_ref, send_ref, inner_ref, outer_ref, mask_ref, sems
):
    copies = [
        pltpu.make_async_copy(a, b, sems.at[i])
        for i, (a, b) in enumerate(
            ((mask_hbm, mask_ref), (inner_hbm, inner_ref), (outer_hbm, outer_ref))
        )
    ]
    for copy in copies:
        copy.start()
    for copy in copies:
        copy.wait()
    core, blk = where_ref[0], where_ref[1]
    for out_ref, slot in ((mine_ref, core), (send_ref, 1 - core)):
        gain = DAMPING * mask_ref[slot, 0].astype(jnp.float32)
        for source, start, count, offset in (
            (inner_ref, 0, 32, blk * 32),
            (outer_ref, 32, 96, 256 + blk * 96),
        ):
            row = lax.broadcasted_iota(jnp.int32, (count, 1024), 0) + offset
            lane = lax.broadcasted_iota(jnp.int32, (count, 1024), 1)
            match = jnp.where(row == lane, 1.0, 0.0)
            out_ref[start : start + count, :] = source[slot, 0] + match * gain


def split_kernel(
    where_ref, mine_ref, recv_ref, keep_ref, send_ref, s1_ref, bulk_ref, es_ref, ei_ref, lee_ref
):
    first = where_ref[0] == 0
    upper = where_ref[2] == 0
    boxes = choose(first, mine_ref[...], recv_ref[...])
    total = boxes[0][0:32, 0:256] + boxes[1][0:32, 0:256]
    s1_ref[0] = total[:, 0:128]
    s1_ref[1] = total[:, 128:256]
    kept = []
    for t, box in enumerate(boxes):
        panels = split_columns(box[:, 256:1024])
        for j in range(6):
            bulk_ref[32 * (6 * t + j) : 32 * (6 * t + j) + 32, :] = panels[j][0:32]
        for j in range(3):
            base = 384 + 144 * t + 48 * j
            bulk_ref[base : base + 48, :] = shared_rows(panels[3 + j][32:128])
            es_ref[t, :, 128 * j : 128 * j + 128] = other_rows(panels[j][32:128])
            lee_ref[t, :, 128 * j : 128 * j + 128] = other_rows(panels[3 + j][32:128])
        ei_ref[t] = other_rows(box[32:128, 0:256])
        kept.append([shared_rows(panels[j][32:128]) for j in range(3)])
    for j in range(3):
        keep_ref[j], send_ref[j] = choose(upper, kept[0][j], kept[1][j])


def first_kernel(early_ref, d_ref):
    for k in range(8):
        for j in range(3):
            at = (slice(48 * k, 48 * k + 48), slice(128 * j, 128 * j + 128))
            for t in range(2):
                d_ref[(t,) + at] = early_ref[8 * t + k, 48 * j : 48 * j + 48]

    def step(kb, carry):
        sweep_refs([d_ref.at[0], d_ref.at[1]], kb)
        return carry

    lax.fori_loop(0, 3, step, 0)
    d_ref[...] = -d_ref[...]


def inner_kernel(where_ref, early_ref, mine_ref, recv_ref, left_ref, inv_ref):
    first = where_ref[0] == 0
    pair = where_ref[2]
    for k in range(8):
        for j in range(2):
            inv_ref[32 * k : 32 * k + 32, 128 * j : 128 * j + 128] = early_ref[
                8 * pair + k, 144 + 32 * j : 176 + 32 * j
            ]

    def step(kb, carry):
        sweep_refs([inv_ref], kb)
        return carry

    lax.fori_loop(0, 2, step, 0)
    boxes = choose(first, mine_ref[32:128, 0:256], recv_ref[32:128, 0:256])
    left_ref[...] = -dot(jnp.concatenate(boxes, 0), inv_ref[...])


def late_kernel(
    where_ref,
    bulk_hbm,
    early_ref,
    d_ref,
    es_ref,
    ei_ref,
    lee_ref,
    left_ref,
    mine_ref,
    recv_ref,
    one_keep_ref,
    one_send_ref,
    two_keep_ref,
    two_send_ref,
    u_ref,
    v_ref,
    c_ref,
    m_ref,
    l_ref,
    t_ref,
    bulk_ref,
    sems,
):
    first = where_ref[0] == 0
    upper = where_ref[2] == 0
    pair = where_ref[2]
    parts = (slice(0, 384), slice(384, 672))
    copies = [
        [
            pltpu.make_async_copy(
                bulk_hbm.at[i, part], bulk_ref.at[i, part], sems.at[16 * h + i]
            )
            for i in range(16)
        ]
        for h, part in enumerate(parts)
    ]
    for group in copies:
        for copy in group:
            copy.start()
    for copy in copies[0]:
        copy.wait()

    def block(i):
        return slice(128 * i, 128 * i + 128)

    for p in range(2):
        for k in range(8):
            at = slice(256 * p + 32 * k, 256 * p + 32 * k + 32)
            for t in range(2):
                for j in range(3):
                    base = 32 * (6 * t + j)
                    u_ref[at, 384 * t + 128 * j : 384 * t + 128 * j + 128] = bulk_ref[
                        8 * p + k, base : base + 32
                    ]


    def fill_v(i):
        for t in range(2):
            cols = slice(384 * t, 384 * t + 384)
            v_ref[block(i), cols] = dot(u_ref[block(i), cols], d_ref[t])

    def fill_c(i):
        width = 128 * (i + 1)
        c_ref[block(i), 0:width] = -dot_nt(v_ref[block(i), :], u_ref[0:width, :])
        p = i // 2
        for k in range(4):
            rows = slice(128 * i + 32 * k, 128 * i + 32 * k + 32)
            for j in range(i % 2 + 1):
                at = 4 * (i % 2) + k
                cols = block(2 * p + j)
                c_ref[rows, cols] = (
                    c_ref[rows, cols] + early_ref[8 * p + at, 144 + 32 * j : 176 + 32 * j]
                )

    def fill_f():
        blank = jnp.zeros((48, 256), jnp.float32)
        for t in range(2):
            placed = jnp.concatenate(choose(upper, ei_ref[t], blank), 1)
            c_ref[512 + 48 * t : 560 + 48 * t, :] = placed - dot_nt(
                es_ref[t], v_ref[:, 384 * t : 384 * t + 384]
            )

    def fill_t():
        for t in range(2):
            t_ref[48 * t : 48 * t + 48, 384 * t : 384 * t + 384] = dot(es_ref[t], d_ref[t])
            t_ref[48 * t : 48 * t + 48, 384 - 384 * t : 768 - 384 * t] = jnp.zeros(
                (48, 384), jnp.float32
            )

    def side(k, rows):
        m_ref[rows, block(k)] = dot(c_ref[rows, block(k)], inverse[k])

    def trail(k, rows, start, stop):
        cols = slice(128 * start, 128 * stop)
        c_ref[rows, cols] = c_ref[rows, cols] - dot_nt(m_ref[rows, block(k)], c_ref[cols, block(k)])


    def fill_one(h, j):
        shared = u_ref[pl.ds(pl.multiple_of(256 * pair, 256), 256), 384 * h + 128 * j : 384 * h + 128 * j + 128]
        base = 32 * (6 * h + 3 + j)
        other = jnp.concatenate(
            [bulk_ref[8 * pair + k, base : base + 32] for k in range(8)], 0
        )
        both = dot(left_ref[...], jnp.concatenate([shared, other], 1))
        halves = join_pair(both[:, 0:128], both[:, 128:256])
        at = 256 * j
        cols = slice(768 * h + at, 768 * h + at + 256)
        rows = []
        for t in range(2):
            part = jnp.concatenate([half[96 * t : 96 * t + 96] for half in halves], 1)
            if t == h:
                natural = jnp.where(
                    first == (t == 0),
                    mine_ref[32:128, 256 + at : 512 + at],
                    recv_ref[32:128, 256 + at : 512 + at],
                )
                rows.append(natural - part)
            else:
                rows.append(-part)
        one_keep_ref[:, cols], one_send_ref[:, cols] = choose(first, rows[0], rows[1])

    def wait_late():
        for copy in copies[1]:
            copy.wait()

    def fill_l(p, t):
        for k in range(8):
            for j in range(3):
                base = 384 + 144 * t + 48 * j
                l_ref[2 * p + t, 48 * k : 48 * k + 48, 128 * j : 128 * j + 128] = bulk_ref[
                    8 * p + k, base : base + 48
                ]
                base = 32 * (6 * t + 3 + j)
                l_ref[2 * p + t, 384 + 32 * k : 416 + 32 * k, 128 * j : 128 * j + 128] = bulk_ref[
                    8 * p + k, base : base + 32
                ]

    inverse = []
    extra = slice(512, 608)
    run = functools.partial
    work = [
        [run(fill_v, 1), run(fill_c, 1)]
        + [run(fill_v, 2), run(fill_c, 2)]
        + [run(fill_v, 3), run(fill_c, 3)]
        + [fill_f, fill_t],
        [
            run(side, 0, slice(256, 608)),
            run(trail, 0, block(2), 1, 3),
            run(trail, 0, block(3), 1, 4),
            run(trail, 0, extra, 1, 4),
        ]
        + [run(fill_one, 0, j) for j in range(3)],
        [
            run(side, 1, slice(384, 608)),
            run(trail, 1, block(3), 2, 4),
            run(trail, 1, extra, 2, 4),
        ]
        + [run(fill_one, 1, j) for j in range(3)],
        [
            run(side, 2, extra),
            run(trail, 2, extra, 3, 4),
            wait_late,
        ]
        + [run(fill_l, p, t) for p in range(2) for t in range(2)],
    ]
    fill_v(0)
    fill_c(0)
    for k in range(4):
        if k:
            side(k - 1, block(k))
            trail(k - 1, block(k), k, k + 1)
        (x,) = sweep_blocks([c_ref[block(k), block(k)]], work[k])
        inverse.append(-x)
    g = [None] * 4
    total = t_ref[...]
    g[3] = dot(c_ref[extra, block(3)], inverse[3])
    for k in (2, 1, 0):
        total = total - dot(g[k + 1], v_ref[block(k + 1), :])
        after = jnp.concatenate(g[k + 1 :], 1)
        g[k] = m_ref[extra, block(k)] - dot(after, m_ref[128 * (k + 1) : 512, block(k)])
    total = total - dot(g[0], v_ref[block(0), :])
    none = jnp.zeros((48, 384), jnp.float32)
    for p in range(2):
        for t in range(2):
            weights = jnp.concatenate([total[:, 384 * t : 384 * t + 384], g[2 * p], g[2 * p + 1]], 1)
            own = jnp.where(pair == p, lee_ref[t], 0.0)
            placed = jnp.concatenate([own, none] if t == 0 else [none, own], 0)
            out = placed - dot(weights, l_ref[2 * p + t])
            cols = slice(384 * (2 * p + t), 384 * (2 * p + t) + 384)
            two_keep_ref[:, cols], two_send_ref[:, cols] = choose(first, out[0:48], out[48:96])


def call(kernel, outs, args, micros, limit, scratch=(), scalars=True, hbm=0):
    shapes = [jax.ShapeDtypeStruct(s, jnp.float32) for s in outs]
    specs = [pl.BlockSpec(memory_space=pltpu.SMEM)] if scalars else []
    specs += [pl.BlockSpec(memory_space=pltpu.HBM)] * hbm
    specs += [pl.BlockSpec(memory_space=pltpu.VMEM)] * (len(args) - len(specs))
    return pl.pallas_call(
        kernel,
        out_shape=shapes,
        in_specs=specs,
        out_specs=[pl.BlockSpec(memory_space=pltpu.VMEM) for _ in outs],
        scratch_shapes=scratch,
        compiler_params=pltpu.CompilerParams(vmem_limit_bytes=limit * 2**20),
        cost_estimate=pl.CostEstimate(
            flops=int(micros * 1e9), bytes_accessed=2**20, transcendentals=0
        ),
    )(*args)


def swap(x, axis):
    return lax.ppermute(x, axis, [(0, 1), (1, 0)])


def by_slot(core, mine, other):
    first = core == 0
    return jnp.stack([jnp.where(first, mine, other), jnp.where(first, other, mine)])[:, None]


def floats(*shape):
    return pltpu.VMEM(shape, jnp.float32)


def local(interface_rows, exterior_rows, pml_mask):
    core = lax.axis_index("core")
    blk = lax.axis_index(("xl", "z"))
    where = jnp.stack([core, blk, lax.axis_index("xh")]).astype(jnp.int32)
    mine, send = call(
        damp_kernel,
        [(128, 1024), (128, 1024)],
        [where, interface_rows, exterior_rows, pml_mask],
        1,
        8,
        hbm=3,
        scratch=[
            floats(2, 1, 32, 1024),
            floats(2, 1, 96, 1024),
            pltpu.VMEM((2, 1, 1024), jnp.int32),
            pltpu.SemaphoreType.DMA((3,)),
        ],
    )
    recv = swap(send, "core")
    keep, away, s1, bulk, es, ei, lee = call(
        split_kernel,
        [
            (3, 48, 128),
            (3, 48, 128),
            (2, 32, 128),
            (672, 128),
            (2, 48, 384),
            (2, 48, 256),
            (2, 48, 384),
        ],
        [where, mine, recv],
        2,
        8,
    )
    bulk_all = lax.all_gather(bulk, PLANE, axis=0, tiled=False)
    shared = keep + swap(away, "xh")
    early = jnp.concatenate([shared.reshape(144, 128), s1.reshape(64, 128)], 0)
    early_all = lax.all_to_all(
        jnp.broadcast_to(early, (16, 208, 128)), PLANE, 0, 0, tiled=False
    )
    (d_inv,) = call(first_kernel, [(2, 384, 384)], [early_all], 17, 12, scalars=False)
    left, _ = call(
        inner_kernel, [(192, 256), (256, 256)], [where, early_all, mine, recv], 8, 8
    )
    one_keep, one_send, two_keep, two_send = call(
        late_kernel,
        [(96, 1536), (96, 1536), (48, 1536), (48, 1536)],
        [where, bulk_all, early_all, d_inv, es, ei, lee, left, mine, recv],
        25,
        48,
        hbm=1,
        scratch=[
            floats(512, 768),
            floats(512, 768),
            floats(608, 512),
            floats(608, 512),
            floats(4, 640, 384),
            floats(96, 768),
            floats(16, 672, 128),
            pltpu.SemaphoreType.DMA((32,)),
        ],
    )
    one_recv = swap(one_send, "core")
    two_recv = swap(two_send, "core")
    return by_slot(core, one_keep, one_recv), by_slot(core, two_keep, two_recv)


def solution(mesh):
    fine = Mesh(mesh.devices.reshape(4, 2, 2, 2, 4), ("y", "xh", "core", "xl", "z"))
    box, blk = ("y", "xh", "core"), ("xl", "z")
    rows = P(None, box, blk, None)
    return jax.shard_map(
        local,
        mesh=fine,
        in_specs=(rows, rows, P(None, box, None)),
        out_specs=(rows, rows),
        check_vma=False,
    )
```

```python
import functools

import jax
import jax.numpy as jnp
from jax import lax
from jax.experimental import pallas as pl
from jax.experimental.pallas import tpu as pltpu
from jax.sharding import Mesh
from jax.sharding import PartitionSpec as P

HI = lax.Precision.HIGHEST
MID = lax.Precision.HIGH
DAMPING = 2.0
PLANE = ("xh", "xl", "z")


def dot(a, b, precision=HI):
    return jnp.dot(a, b, precision=precision, preferred_element_type=jnp.float32)


def dot_nt(a, b, precision=HI):
    return lax.dot_general(
        a, b, (((1,), (1,)), ((), ())), precision=precision, preferred_element_type=jnp.float32
    )


def dot_tn(a, b):
    return lax.dot_general(
        a, b, (((0,), (0,)), ((), ())), precision=HI, preferred_element_type=jnp.float32
    )


PANEL = 16


def tree_sum(t):
    while len(t) > 1:
        t = [t[i] + t[i + 1] for i in range(0, len(t) - 1, 2)] + ([t[-1]] if len(t) % 2 else [])
    return t[0]


def spread_lane(x, at):
    return jnp.broadcast_to(x[:, at : at + 1], x.shape)


def spread_row(x, at):
    return jnp.broadcast_to(x[at : at + 1], x.shape)


def eliminate(rows, base, lane, sub):
    count = 8 * len(rows)
    cols = [[spread_lane(x, base + q) for x in rows] for q in range(count)]
    inblk = (lane >= base) & (lane < base + count)
    out = [
        jnp.where(inblk, jnp.where(lane == sub + (8 * v + base), -1.0, 0.0), x)
        for v, x in enumerate(rows)
    ]
    scale = 1.0 / spread_row(cols[0][0], 0)
    for k in range(count):
        kv, ks = divmod(k, 8)
        hit = sub == ks
        if k + 1 < count:
            nv, ns = divmod(k + 1, 8)
            over = spread_row(cols[k + 1][kv], ks) * scale
            pivot = spread_row(cols[k + 1][nv], ns) - spread_row(cols[k][nv], ns) * over
            ahead = 1.0 / pivot

        def update(tiles):
            row = spread_row(tiles[kv], ks) * scale
            new = [x - c * row for x, c in zip(tiles, cols[k])]
            new[kv] = jnp.where(hit, row, new[kv])
            return new

        for j in range(k + 1, count):
            cols[j] = update(cols[j])
        out = update(out)
        if k + 1 < count:
            scale = ahead
    return out


def sweep_blocks(mats, work=()):
    work = list(work)
    tiles, per = 16, PANEL // 8
    lane = lax.broadcasted_iota(jnp.int32, (8, 128), 1)
    sub = lax.broadcasted_iota(jnp.int32, (8, 128), 0)
    mats = [[a[8 * i : 8 * i + 8] for i in range(tiles)] for a in mats]
    for k in range(tiles // per):
        base = PANEL * k
        inblk = (lane >= base) & (lane < base + PANEL)
        own = range(per * k, per * k + per)
        near = range(per * k + per, min(per * k + 2 * per, tiles))
        for c, rows in enumerate(mats):
            cols = {t: [spread_lane(rows[t], base + q) for q in range(PANEL)] for t in near}
            solved = eliminate([rows[t] for t in own], base, lane, sub)
            new = list(rows)
            if near:
                each = [spread_row(solved[q // 8], q % 8) for q in range(PANEL)]
                for t in near:
                    total = tree_sum([cols[t][q] * each[q] for q in range(PANEL)])
                    new[t] = jnp.where(inblk, 0.0, rows[t]) - total
            change = dot_tn(
                jnp.concatenate([rows[t] for t in own], 0), jnp.concatenate(solved, 0)
            )
            for t in range(tiles):
                if t in own:
                    new[t] = solved[t - per * k]
                elif t not in near:
                    new[t] = jnp.where(inblk, 0.0, rows[t]) - change[8 * t : 8 * t + 8]
            mats[c] = new
        left = tiles // per - k
        for _ in range(-(-len(work) // left)):
            work.pop(0)()
    return [jnp.concatenate(rows, 0) for rows in mats]


def lane_index(rows, back):
    lane = lax.broadcasted_iota(jnp.int32, (rows, 128), 1)
    if back:
        seg = lane // 16
        return (seg % 2) * 64 + (seg // 2) * 16 + lane % 16
    half = lane // 64
    return ((lane % 64) // 16) * 32 + half * 16 + lane % 16


def pick(x, index):
    return jnp.take_along_axis(x, index, axis=1)


def split_columns(x):
    rows = x.shape[0]
    index = lane_index(rows, False)
    low = lax.broadcasted_iota(jnp.int32, (rows, 128), 1) < 64
    shared, other = [], []
    for j in range(3):
        a = pick(x[:, 256 * j : 256 * j + 128], index)
        b = pick(x[:, 256 * j + 128 : 256 * j + 256], index)
        shared.append(jnp.where(low, a, pltpu.roll(b, 64, 1)))
        other.append(jnp.where(low, pltpu.roll(a, 64, 1), b))
    return shared + other


def join_pair(shared, other):
    rows = shared.shape[0]
    index = lane_index(rows, True)
    low = lax.broadcasted_iota(jnp.int32, (rows, 128), 1) < 64
    return (
        pick(jnp.where(low, shared, pltpu.roll(other, 64, 1)), index),
        pick(jnp.where(low, pltpu.roll(shared, 64, 1), other), index),
    )


def shared_rows(x):
    return jnp.concatenate([x[0:16], x[32:48], x[64:80]], 0)


def other_rows(x):
    return jnp.concatenate([x[16:32], x[48:64], x[80:96]], 0)


def choose(first, a, b):
    return jnp.where(first, a, b), jnp.where(first, b, a)


def split_kernel(
    where_ref, mine_ref, recv_ref, keep_ref, send_ref, s1_ref, bulk_ref, es_ref, ei_ref, lee_ref
):
    first = where_ref[0] == 0
    upper = where_ref[2] == 0
    boxes = choose(first, mine_ref[...], recv_ref[...])
    total = boxes[0][0:32, 0:256] + boxes[1][0:32, 0:256]
    s1_ref[0] = total[:, 0:128]
    s1_ref[1] = total[:, 128:256]
    kept = []
    blocks = [(where_ref[1] * 48 + 16 * s) // 128 for s in range(3)]
    for t, box in enumerate(boxes):
        panels = split_columns(box[:, 256:1024])
        for j in range(6):
            base = 32 * (3 * t + j % 3) + 192 * (j // 3)
            bulk_ref[base : base + 32, :] = panels[j][0:32]
        for j in range(3):
            base = 384 + 144 * t + 48 * j
            bulk_ref[base : base + 48, :] = shared_rows(panels[3 + j][32:128])
            es_ref[t, :, 128 * j : 128 * j + 128] = other_rows(panels[j][32:128])
            lee_ref[t, :, 128 * j : 128 * j + 128] = other_rows(panels[3 + j][32:128])
        ei_ref[t] = other_rows(box[32:128, 0:256])
        kept.append([shared_rows(panels[j][32:128]) for j in range(3)])
    for s, i in enumerate(blocks):
        rows = slice(16 * s, 16 * s + 16)
        for step in range(2):
            tiles = []
            for t in range(2):
                a, b, c = (kept[t][(j + step) % 3][rows] for j in range(3))
                tiles.append(jnp.where(i == 0, a, jnp.where(i == 1, b, c)))
            keep_ref[step, rows], send_ref[step, rows] = choose(upper, *tiles)


def first_kernel(
    where_ref,
    x0_ref,
    x1_ref,
    x2_ref,
    x3_ref,
    mine_ref,
    recv_ref,
    d_ref,
    s1_ref,
    left_ref,
    s_ref,
    e_ref,
):
    first = where_ref[0] == 0
    pair, x, z = where_ref[2], where_ref[3], where_ref[4]
    for turn, ref in enumerate((x0_ref, x1_ref, x2_ref, x3_ref)):
        for shift in range(4):
            source = lax.rem(x + 4 - shift, 4)
            half, low = source // 2, lax.rem(source, 2)
            k = low * 4 + lax.rem(z + 4 - turn, 4)
            rows = pl.ds(pl.multiple_of(48 * k, 16), 48)
            for j in range(2):
                e_ref[half, rows, 128 * j : 128 * j + 128] = ref[shift, 48 * j : 48 * j + 48]
            rows = pl.ds(pl.multiple_of(32 * k, 32), 32)
            for j in range(2):
                s1_ref[half, rows, 128 * j : 128 * j + 128] = ref[
                    shift, 96 + 32 * j : 128 + 32 * j
                ]
    s_ref[...] = s1_ref[pair]
    mats = [e_ref.at[0], e_ref.at[1], s_ref]
    both = range(2)

    def at(i, j):
        return slice(128 * i, 128 * i + 128), slice(128 * j, 128 * j + 128)

    def inverses(blocks, work=()):
        return [-x for x in sweep_blocks(blocks, work)]

    x0 = inverses([ref[at(0, 0)] for ref in mats])
    a01 = [ref[at(0, 1)] for ref in mats]
    m1 = [dot_tn(a, x) for a, x in zip(a01, x0)]
    corners = [ref[at(1, 0)] for ref in mats[:2]] + [s_ref[at(1, 1)]]
    a11 = [c - dot(m, a) for c, m, a in zip(corners, m1, a01)]
    m2, a21, a22, p2, b00, b10 = ([None] * 2 for _ in range(6))

    def third_rows(c):
        a20 = mats[c][at(2, 1)]
        m2[c] = dot(a20, x0[c])
        a21[c] = mats[c][at(1, 1)].T - dot(m2[c], a01[c])
        a22[c] = mats[c][at(2, 0)] - dot_nt(m2[c], a20)

    x1 = inverses(a11, [functools.partial(third_rows, c) for c in both])
    n2 = [dot(a21[c], x1[c]) for c in both]
    last = [a22[c] - dot_nt(n2[c], a21[c]) for c in both]

    def two_by_two(c):
        q = dot(x1[c], m1[c])
        return x0[c] + dot_tn(m1[c], q), -q

    def corner(c):
        p2[c] = m2[c] - dot(n2[c], m1[c])
        b00[c], b10[c] = two_by_two(c)

    def interface():
        s00, s10 = two_by_two(2)
        s_ref[at(0, 0)] = s00
        s_ref[at(1, 0)] = s10
        s_ref[at(0, 1)] = s10.T
        s_ref[at(1, 1)] = x1[2]

    def weights():
        boxes = choose(first, mine_ref[32:128, 0:256], recv_ref[32:128, 0:256])
        left_ref[...] = dot(jnp.concatenate(boxes, 0), s_ref[...])

    x2 = inverses(last, [functools.partial(corner, c) for c in both] + [interface, weights])
    for c in both:
        ref = d_ref.at[c]
        q0, q1 = dot(x2[c], p2[c]), dot(x2[c], n2[c])
        mid = b10[c] + dot_tn(n2[c], q0)
        ref[at(0, 0)] = b00[c] + dot_tn(p2[c], q0)
        ref[at(1, 0)] = mid
        ref[at(0, 1)] = mid.T
        ref[at(1, 1)] = x1[c] + dot_tn(n2[c], q1)
        ref[at(2, 0)] = -q0
        ref[at(0, 2)] = -q0.T
        ref[at(2, 1)] = -q1
        ref[at(1, 2)] = -q1.T
        ref[at(2, 2)] = x2[c]


def late_kernel(
    where_ref,
    bulk_hbm,
    s1_ref,
    d_ref,
    es_ref,
    ei_ref,
    lee_ref,
    left_ref,
    mine_ref,
    recv_ref,
    one_keep_ref,
    one_send_ref,
    two_keep_ref,
    two_send_ref,
    u_ref,
    v_ref,
    c_ref,
    m_ref,
    l_ref,
    t_ref,
    bulk_ref,
    sems,
):
    first = where_ref[0] == 0
    upper = where_ref[2] == 0
    pair = where_ref[2]
    parts = (slice(0, 192), slice(192, 672))
    copies = [
        [
            pltpu.make_async_copy(
                bulk_hbm.at[i, part], bulk_ref.at[i, part], sems.at[16 * h + i]
            )
            for i in range(16)
        ]
        for h, part in enumerate(parts)
    ]
    for group in copies:
        for copy in group:
            copy.start()
    for copy in copies[0]:
        copy.wait()

    def block(i):
        return slice(128 * i, 128 * i + 128)

    for p in range(2):
        for k in range(8):
            at = slice(256 * p + 32 * k, 256 * p + 32 * k + 32)
            for t in range(2):
                for j in range(3):
                    base = 32 * (3 * t + j)
                    u_ref[at, 384 * t + 128 * j : 384 * t + 128 * j + 128] = bulk_ref[
                        8 * p + k, base : base + 32
                    ]


    def fill_v(i):
        for t in range(2):
            cols = slice(384 * t, 384 * t + 384)
            v_ref[block(i), cols] = dot(u_ref[block(i), cols], d_ref[t])

    def fill_c(i):
        width = 128 * (i + 1)
        c_ref[block(i), 0:width] = -dot_nt(v_ref[block(i), :], u_ref[0:width, :], MID)
        p = i // 2
        cols = slice(256 * p, width)
        c_ref[block(i), cols] = (
            c_ref[block(i), cols] + s1_ref[p, block(i % 2), 0 : width - 256 * p]
        )

    def fill_f():
        blank = jnp.zeros((48, 256), jnp.float32)
        for t in range(2):
            placed = jnp.concatenate(choose(upper, ei_ref[t], blank), 1)
            c_ref[512 + 48 * t : 560 + 48 * t, :] = placed - dot_nt(
                es_ref[t], v_ref[:, 384 * t : 384 * t + 384], MID
            )

    def fill_t():
        for t in range(2):
            t_ref[48 * t : 48 * t + 48, 384 * t : 384 * t + 384] = dot(es_ref[t], d_ref[t])
            t_ref[48 * t : 48 * t + 48, 384 - 384 * t : 768 - 384 * t] = jnp.zeros(
                (48, 384), jnp.float32
            )

    def side(k, rows):
        m_ref[rows, block(k)] = dot(c_ref[rows, block(k)], inverse[k])

    def trail(k, rows, start, stop):
        cols = slice(128 * start, 128 * stop)
        c_ref[rows, cols] = c_ref[rows, cols] - dot_nt(m_ref[rows, block(k)], c_ref[cols, block(k)])


    def fill_one(h, j):
        shared = u_ref[pl.ds(pl.multiple_of(256 * pair, 256), 256), 384 * h + 128 * j : 384 * h + 128 * j + 128]
        base = 192 + 32 * (3 * h + j)
        other = jnp.concatenate(
            [bulk_ref[8 * pair + k, base : base + 32] for k in range(8)], 0
        )
        both = dot(left_ref[...], jnp.concatenate([shared, other], 1), MID)
        halves = join_pair(both[:, 0:128], both[:, 128:256])
        at = 256 * j
        cols = slice(768 * h + at, 768 * h + at + 256)
        rows = []
        for t in range(2):
            part = jnp.concatenate([half[96 * t : 96 * t + 96] for half in halves], 1)
            if t == h:
                natural = jnp.where(
                    first == (t == 0),
                    mine_ref[32:128, 256 + at : 512 + at],
                    recv_ref[32:128, 256 + at : 512 + at],
                )
                rows.append(natural - part)
            else:
                rows.append(-part)
        one_keep_ref[:, cols], one_send_ref[:, cols] = choose(first, rows[0], rows[1])

    def wait_late():
        for copy in copies[1]:
            copy.wait()

    def fill_l(p, t):
        for k in range(8):
            for j in range(3):
                base = 384 + 144 * t + 48 * j
                l_ref[2 * p + t, 48 * k : 48 * k + 48, 128 * j : 128 * j + 128] = bulk_ref[
                    8 * p + k, base : base + 48
                ]
                base = 192 + 32 * (3 * t + j)
                l_ref[2 * p + t, 384 + 32 * k : 416 + 32 * k, 128 * j : 128 * j + 128] = bulk_ref[
                    8 * p + k, base : base + 32
                ]

    inverse = []
    extra = slice(512, 608)
    run = functools.partial
    work = [
        [run(fill_v, 1), run(fill_c, 1)]
        + [run(fill_v, 2), run(fill_c, 2)]
        + [run(fill_v, 3), run(fill_c, 3)]
        + [fill_f, fill_t],
        [
            run(side, 0, slice(256, 608)),
            run(trail, 0, block(2), 1, 3),
            run(trail, 0, block(3), 1, 4),
            run(trail, 0, extra, 1, 4),
            wait_late,
        ]
        + [run(fill_one, 0, j) for j in range(3)],
        [
            run(side, 1, slice(384, 608)),
            run(trail, 1, block(3), 2, 4),
            run(trail, 1, extra, 2, 4),
        ]
        + [run(fill_one, 1, j) for j in range(3)],
        [
            run(side, 2, extra),
            run(trail, 2, extra, 3, 4),
        ]
        + [run(fill_l, p, t) for p in range(2) for t in range(2)],
    ]
    fill_v(0)
    fill_c(0)
    for k in range(4):
        if k:
            side(k - 1, block(k))
            trail(k - 1, block(k), k, k + 1)
        (x,) = sweep_blocks([c_ref[block(k), block(k)]], work[k])
        inverse.append(-x)
    g = [None] * 4
    total = t_ref[...]
    g[3] = dot(c_ref[extra, block(3)], inverse[3])
    for k in (2, 1, 0):
        total = total - dot(g[k + 1], v_ref[block(k + 1), :], MID)
        after = jnp.concatenate(g[k + 1 :], 1)
        g[k] = m_ref[extra, block(k)] - dot(after, m_ref[128 * (k + 1) : 512, block(k)])
    total = total - dot(g[0], v_ref[block(0), :], MID)
    none = jnp.zeros((48, 384), jnp.float32)
    for p in range(2):
        for t in range(2):
            weights = jnp.concatenate([total[:, 384 * t : 384 * t + 384], g[2 * p], g[2 * p + 1]], 1)
            own = jnp.where(pair == p, lee_ref[t], 0.0)
            placed = jnp.concatenate([own, none] if t == 0 else [none, own], 0)
            out = placed - dot(weights, l_ref[2 * p + t], MID)
            cols = slice(384 * (2 * p + t), 384 * (2 * p + t) + 384)
            two_keep_ref[:, cols], two_send_ref[:, cols] = choose(first, out[0:48], out[48:96])


def call(kernel, outs, args, micros, limit, scratch=(), scalars=True, hbm=0):
    shapes = [jax.ShapeDtypeStruct(s, jnp.float32) for s in outs]
    specs = [pl.BlockSpec(memory_space=pltpu.SMEM)] if scalars else []
    specs += [pl.BlockSpec(memory_space=pltpu.HBM)] * hbm
    specs += [pl.BlockSpec(memory_space=pltpu.VMEM)] * (len(args) - len(specs))
    return pl.pallas_call(
        kernel,
        out_shape=shapes,
        in_specs=specs,
        out_specs=[pl.BlockSpec(memory_space=pltpu.VMEM) for _ in outs],
        scratch_shapes=scratch,
        compiler_params=pltpu.CompilerParams(vmem_limit_bytes=limit * 2**20),
        cost_estimate=pl.CostEstimate(
            flops=int(micros * 1e9), bytes_accessed=2**20, transcendentals=0
        ),
    )(*args)


def swap(x, axis):
    return lax.ppermute(x, axis, [(0, 1), (1, 0)])


def by_slot(core, mine, other):
    first = core == 0
    return jnp.stack([jnp.where(first, mine, other), jnp.where(first, other, mine)])[:, None]


def floats(*shape):
    return pltpu.VMEM(shape, jnp.float32)


def damped(rows, offset, gain):
    count, width = rows.shape
    row = lax.broadcasted_iota(jnp.int32, (count, width), 0) + offset
    lane = lax.broadcasted_iota(jnp.int32, (count, width), 1)
    return rows + jnp.where(row == lane, gain[None, :], 0.0)


def shift_by(x, axis, step):
    return lax.ppermute(x, axis, [(i, (i + step) % 4) for i in range(4)])


def local(interface_rows, exterior_rows, pml_mask):
    core = lax.axis_index("core")
    blk = lax.axis_index(("xl", "z"))
    where = jnp.stack(
        [core, blk, lax.axis_index("xh"), lax.axis_index(("xh", "xl")), lax.axis_index("z")]
    ).astype(jnp.int32)

    def slot_rows(second):
        inner, outer, mask = (
            jnp.where(second, a[1, 0], a[0, 0]) for a in (interface_rows, exterior_rows, pml_mask)
        )
        gain = DAMPING * mask.astype(jnp.float32)
        return jnp.concatenate(
            [damped(inner, blk * 32, gain), damped(outer, 256 + blk * 96, gain)], 0
        )

    send = slot_rows(core == 0)
    recv = swap(send, "core")
    mine = slot_rows(core == 1)
    keep, away, s1, bulk, es, ei, lee = call(
        split_kernel,
        [
            (2, 48, 128),
            (2, 48, 128),
            (2, 32, 128),
            (672, 128),
            (2, 48, 384),
            (2, 48, 256),
            (2, 48, 384),
        ],
        [where, mine, recv],
        2,
        8,
    )
    bulk_all = lax.all_gather(bulk, PLANE, axis=0, tiled=False)
    shared = keep + swap(away, "xh")
    early = jnp.concatenate([shared.reshape(96, 128), s1.reshape(64, 128)], 0)
    line = jnp.stack([early] + [shift_by(early, ("xh", "xl"), d) for d in (1, 2, 3)])
    plane = [line] + [shift_by(line, "z", d) for d in (1, 2, 3)]
    d_inv, s1_all, left = call(
        first_kernel,
        [(2, 384, 384), (2, 256, 256), (192, 256)],
        [where, *plane, mine, recv],
        20,
        12,
        scratch=[floats(256, 256), floats(2, 384, 256)],
    )
    one_keep, one_send, two_keep, two_send = call(
        late_kernel,
        [(96, 1536), (96, 1536), (48, 1536), (48, 1536)],
        [where, bulk_all, s1_all, d_inv, es, ei, lee, left, mine, recv],
        25,
        48,
        hbm=1,
        scratch=[
            floats(512, 768),
            floats(512, 768),
            floats(608, 512),
            floats(608, 512),
            floats(4, 640, 384),
            floats(96, 768),
            floats(16, 672, 128),
            pltpu.SemaphoreType.DMA((32,)),
        ],
    )
    one_recv = swap(one_send, "core")
    two_recv = swap(two_send, "core")
    return by_slot(core, one_keep, one_recv), by_slot(core, two_keep, two_recv)


def solution(mesh):
    fine = Mesh(mesh.devices.reshape(4, 2, 2, 2, 4), ("y", "xh", "core", "xl", "z"))
    box, blk = ("y", "xh", "core"), ("xl", "z")
    rows = P(None, box, blk, None)
    return jax.shard_map(
        local,
        mesh=fine,
        in_specs=(rows, rows, P(None, box, None)),
        out_specs=(rows, rows),
        check_vma=False,
    )
```

```python
import functools

import jax
import jax.numpy as jnp
from jax import lax
from jax.experimental import pallas as pl
from jax.experimental.pallas import tpu as pltpu
from jax.sharding import Mesh
from jax.sharding import PartitionSpec as P

HI = lax.Precision.HIGHEST
MID = lax.Precision.HIGH
DAMPING = 2.0
PLANE = ("xh", "xl", "z")


def dot(a, b, precision=HI):
    return jnp.dot(a, b, precision=precision, preferred_element_type=jnp.float32)


def dot_nt(a, b, precision=HI):
    return lax.dot_general(
        a, b, (((1,), (1,)), ((), ())), precision=precision, preferred_element_type=jnp.float32
    )


def dot_tn(a, b):
    return lax.dot_general(
        a, b, (((0,), (0,)), ((), ())), precision=HI, preferred_element_type=jnp.float32
    )


PANEL = 16


def tree_sum(t):
    while len(t) > 1:
        t = [t[i] + t[i + 1] for i in range(0, len(t) - 1, 2)] + ([t[-1]] if len(t) % 2 else [])
    return t[0]


def spread_lane(x, at):
    return jnp.broadcast_to(x[:, at : at + 1], x.shape)


def spread_row(x, at):
    return jnp.broadcast_to(x[at : at + 1], x.shape)


def eliminate(rows, base, lane, sub):
    count = 8 * len(rows)
    cols = [[spread_lane(x, base + q) for x in rows] for q in range(count)]
    inblk = (lane >= base) & (lane < base + count)
    out = [
        jnp.where(inblk, jnp.where(lane == sub + (8 * v + base), -1.0, 0.0), x)
        for v, x in enumerate(rows)
    ]
    scale = 1.0 / spread_row(cols[0][0], 0)
    for k in range(count):
        kv, ks = divmod(k, 8)
        hit = sub == ks
        if k + 1 < count:
            nv, ns = divmod(k + 1, 8)
            over = spread_row(cols[k + 1][kv], ks) * scale
            pivot = spread_row(cols[k + 1][nv], ns) - spread_row(cols[k][nv], ns) * over
            ahead = 1.0 / pivot

        def update(tiles):
            row = spread_row(tiles[kv], ks) * scale
            new = [x - c * row for x, c in zip(tiles, cols[k])]
            new[kv] = jnp.where(hit, row, new[kv])
            return new

        for j in range(k + 1, count):
            cols[j] = update(cols[j])
        out = update(out)
        if k + 1 < count:
            scale = ahead
    return out


def sweep_blocks(mats, work=()):
    work = list(work)
    tiles, per = 16, PANEL // 8
    lane = lax.broadcasted_iota(jnp.int32, (8, 128), 1)
    sub = lax.broadcasted_iota(jnp.int32, (8, 128), 0)
    mats = [[a[8 * i : 8 * i + 8] for i in range(tiles)] for a in mats]
    for k in range(tiles // per):
        base = PANEL * k
        inblk = (lane >= base) & (lane < base + PANEL)
        own = range(per * k, per * k + per)
        near = range(per * k + per, min(per * k + 2 * per, tiles))
        for c, rows in enumerate(mats):
            cols = {t: [spread_lane(rows[t], base + q) for q in range(PANEL)] for t in near}
            solved = eliminate([rows[t] for t in own], base, lane, sub)
            new = list(rows)
            if near:
                each = [spread_row(solved[q // 8], q % 8) for q in range(PANEL)]
                for t in near:
                    total = tree_sum([cols[t][q] * each[q] for q in range(PANEL)])
                    new[t] = jnp.where(inblk, 0.0, rows[t]) - total
            change = dot_tn(
                jnp.concatenate([rows[t] for t in own], 0), jnp.concatenate(solved, 0)
            )
            for t in range(tiles):
                if t in own:
                    new[t] = solved[t - per * k]
                elif t not in near:
                    new[t] = jnp.where(inblk, 0.0, rows[t]) - change[8 * t : 8 * t + 8]
            mats[c] = new
        left = tiles // per - k
        for _ in range(-(-len(work) // left)):
            work.pop(0)()
    return [jnp.concatenate(rows, 0) for rows in mats]


def lane_index(rows, back):
    lane = lax.broadcasted_iota(jnp.int32, (rows, 128), 1)
    if back:
        seg = lane // 16
        return (seg % 2) * 64 + (seg // 2) * 16 + lane % 16
    half = lane // 64
    return ((lane % 64) // 16) * 32 + half * 16 + lane % 16


def pick(x, index):
    return jnp.take_along_axis(x, index, axis=1)


def split_columns(x):
    rows = x.shape[0]
    index = lane_index(rows, False)
    low = lax.broadcasted_iota(jnp.int32, (rows, 128), 1) < 64
    shared, other = [], []
    for j in range(3):
        a = pick(x[:, 256 * j : 256 * j + 128], index)
        b = pick(x[:, 256 * j + 128 : 256 * j + 256], index)
        shared.append(jnp.where(low, a, pltpu.roll(b, 64, 1)))
        other.append(jnp.where(low, pltpu.roll(a, 64, 1), b))
    return shared + other


def join_pair(shared, other):
    rows = shared.shape[0]
    index = lane_index(rows, True)
    low = lax.broadcasted_iota(jnp.int32, (rows, 128), 1) < 64
    return (
        pick(jnp.where(low, shared, pltpu.roll(other, 64, 1)), index),
        pick(jnp.where(low, pltpu.roll(shared, 64, 1), other), index),
    )


def shared_rows(x):
    return jnp.concatenate([x[0:16], x[32:48], x[64:80]], 0)


def other_rows(x):
    return jnp.concatenate([x[16:32], x[48:64], x[80:96]], 0)


def choose(first, a, b):
    return jnp.where(first, a, b), jnp.where(first, b, a)


def split_kernel(
    where_ref, mine_ref, recv_ref, keep_ref, send_ref, s1_ref, bulk_ref, es_ref, ei_ref, lee_ref
):
    first = where_ref[0] == 0
    upper = where_ref[2] == 0
    boxes = choose(first, mine_ref[...], recv_ref[...])
    total = boxes[0][0:32, 0:256] + boxes[1][0:32, 0:256]
    s1_ref[0] = total[:, 0:128]
    s1_ref[1] = total[:, 128:256]
    kept = []
    blocks = [(where_ref[1] * 48 + 16 * s) // 128 for s in range(3)]
    for t, box in enumerate(boxes):
        panels = split_columns(box[:, 256:1024])
        for j in range(6):
            base = 32 * (3 * t + j % 3) + 192 * (j // 3)
            bulk_ref[base : base + 32, :] = panels[j][0:32]
        for j in range(3):
            base = 384 + 144 * t + 48 * j
            bulk_ref[base : base + 48, :] = shared_rows(panels[3 + j][32:128])
            es_ref[t, :, 128 * j : 128 * j + 128] = other_rows(panels[j][32:128])
            lee_ref[t, :, 128 * j : 128 * j + 128] = other_rows(panels[3 + j][32:128])
        ei_ref[t] = other_rows(box[32:128, 0:256])
        kept.append([shared_rows(panels[j][32:128]) for j in range(3)])
    for s, i in enumerate(blocks):
        rows = slice(16 * s, 16 * s + 16)
        for step in range(2):
            tiles = []
            for t in range(2):
                a, b, c = (kept[t][(j + step) % 3][rows] for j in range(3))
                tiles.append(jnp.where(i == 0, a, jnp.where(i == 1, b, c)))
            keep_ref[step, rows], send_ref[step, rows] = choose(upper, *tiles)


def first_kernel(
    where_ref,
    x0_ref,
    x1_ref,
    x2_ref,
    x3_ref,
    mine_ref,
    recv_ref,
    es_ref,
    dd_ref,
    s1_ref,
    left_ref,
    s_ref,
    e_ref,
):
    first = where_ref[0] == 0
    pair, x, z = where_ref[2], where_ref[3], where_ref[4]
    d_ref, direct_ref = dd_ref.at[:, 0:384], dd_ref.at[:, 384:432]
    for turn, ref in enumerate((x0_ref, x1_ref, x2_ref, x3_ref)):
        for shift in range(4):
            source = lax.rem(x + 4 - shift, 4)
            half, low = source // 2, lax.rem(source, 2)
            k = low * 4 + lax.rem(z + 4 - turn, 4)
            rows = pl.ds(pl.multiple_of(48 * k, 16), 48)
            for j in range(2):
                e_ref[half, rows, 128 * j : 128 * j + 128] = ref[shift, 48 * j : 48 * j + 48]
            rows = pl.ds(pl.multiple_of(32 * k, 32), 32)
            for j in range(2):
                s1_ref[half, rows, 128 * j : 128 * j + 128] = ref[
                    shift, 96 + 32 * j : 128 + 32 * j
                ]
    s_ref[...] = s1_ref[pair]
    mats = [e_ref.at[0], e_ref.at[1], s_ref]
    both = range(2)

    def at(i, j):
        return slice(128 * i, 128 * i + 128), slice(128 * j, 128 * j + 128)

    def inverses(blocks, work=()):
        return [-x for x in sweep_blocks(blocks, work)]

    x0 = inverses([ref[at(0, 0)] for ref in mats])
    a01 = [ref[at(0, 1)] for ref in mats]
    m1 = [dot_tn(a, x) for a, x in zip(a01, x0)]
    corners = [ref[at(1, 0)] for ref in mats[:2]] + [s_ref[at(1, 1)]]
    a11 = [c - dot(m, a) for c, m, a in zip(corners, m1, a01)]
    m2, a21, a22, p2, b00, b10 = ([None] * 2 for _ in range(6))

    def third_rows(c):
        a20 = mats[c][at(2, 1)]
        m2[c] = dot(a20, x0[c])
        a21[c] = mats[c][at(1, 1)].T - dot(m2[c], a01[c])
        a22[c] = mats[c][at(2, 0)] - dot_nt(m2[c], a20)

    x1 = inverses(a11, [functools.partial(third_rows, c) for c in both])
    n2 = [dot(a21[c], x1[c]) for c in both]
    last = [a22[c] - dot_nt(n2[c], a21[c]) for c in both]

    def two_by_two(c):
        q = dot(x1[c], m1[c])
        return x0[c] + dot_tn(m1[c], q), -q

    def corner(c):
        p2[c] = m2[c] - dot(n2[c], m1[c])
        b00[c], b10[c] = two_by_two(c)

    def interface():
        s00, s10 = two_by_two(2)
        s_ref[at(0, 0)] = s00
        s_ref[at(1, 0)] = s10
        s_ref[at(0, 1)] = s10.T
        s_ref[at(1, 1)] = x1[2]

    def weights():
        boxes = choose(first, mine_ref[32:128, 0:256], recv_ref[32:128, 0:256])
        for t in range(2):
            left_ref[t] = dot(boxes[t], s_ref[...])

    x2 = inverses(last, [functools.partial(corner, c) for c in both] + [interface, weights])
    for c in both:
        ref = d_ref.at[c]
        q0, q1 = dot(x2[c], p2[c]), dot(x2[c], n2[c])
        mid = b10[c] + dot_tn(n2[c], q0)
        ref[at(0, 0)] = b00[c] + dot_tn(p2[c], q0)
        ref[at(1, 0)] = mid
        ref[at(0, 1)] = mid.T
        ref[at(1, 1)] = x1[c] + dot_tn(n2[c], q1)
        ref[at(2, 0)] = -q0
        ref[at(0, 2)] = -q0.T
        ref[at(2, 1)] = -q1
        ref[at(1, 2)] = -q1.T
        ref[at(2, 2)] = x2[c]
        direct_ref[c] = dot(es_ref[c], ref[...])


def late_kernel(
    where_ref,
    bulk_hbm,
    dd_ref,
    s1_ref,
    left_ref,
    ei_ref,
    lee_ref,
    mine_ref,
    recv_ref,
    one_ref,
    one_send_ref,
    two_ref,
    two_send_ref,
    u_ref,
    ut_ref,
    v_ref,
    c_ref,
    m_ref,
    l_ref,
    t_ref,
    bulk_ref,
    sems,
):
    first = where_ref[0] == 0
    upper = where_ref[2] == 0
    pair = where_ref[2]
    d_ref, direct_ref = dd_ref.at[:, 0:384], dd_ref.at[:, 384:432]
    parts = (slice(0, 192), slice(192, 672))
    copies = [
        [
            pltpu.make_async_copy(
                bulk_hbm.at[i, part], bulk_ref.at[i, part], sems.at[16 * h + i]
            )
            for i in range(16)
        ]
        for h, part in enumerate(parts)
    ]
    for group in copies:
        for copy in group:
            copy.start()
    for copy in copies[0]:
        copy.wait()

    def block(i):
        return slice(128 * i, 128 * i + 128)

    for p in range(2):
        for k in range(8):
            at = slice(256 * p + 32 * k, 256 * p + 32 * k + 32)
            for t in range(2):
                for j in range(3):
                    base = 32 * (3 * t + j)
                    u_ref[at, 384 * t + 128 * j : 384 * t + 128 * j + 128] = bulk_ref[
                        8 * p + k, base : base + 32
                    ]


    head, rest = slice(0, 128), slice(128, 512)

    def fill_v(rows, t):
        cols = slice(384 * t, 384 * t + 384)
        v_ref[rows, cols] = dot(u_ref[rows, cols], d_ref[t])

    def fill_ut(i):
        ut_ref[:, block(i)] = u_ref[block(i), :].T

    def fill_c(rows, width):
        c_ref[rows, 0:width] = -dot(v_ref[rows, :], ut_ref[:, 0:width], MID)

    def add_s1(rows, p):
        cols = slice(256 * p, 256 * p + 256)
        start = rows.start - 256 * p
        c_ref[rows, cols] = c_ref[rows, cols] + s1_ref[p, start : start + rows.stop - rows.start, :]

    def fill_f():
        blank = jnp.zeros((48, 256), jnp.float32)
        none = jnp.zeros((48, 384), jnp.float32)
        for t in range(2):
            rows, cols = slice(48 * t, 48 * t + 48), slice(384 * t, 384 * t + 384)
            placed = jnp.concatenate(choose(upper, ei_ref[t], blank), 1)
            c_ref[512 + 48 * t : 560 + 48 * t, :] = placed - dot(
                direct_ref[t], ut_ref[cols, :], MID
            )
            t_ref[rows, cols] = direct_ref[t]
            t_ref[rows, 384 - 384 * t : 768 - 384 * t] = none

    def fill_rest():
        fill_c(rest, 512)
        add_s1(slice(128, 256), 0)
        add_s1(slice(256, 512), 1)

    def side(k, rows):
        m_ref[rows, block(k)] = dot(c_ref[rows, block(k)], inverse[k])

    def trail(k, rows, start, stop):
        cols = slice(128 * start, 128 * stop)
        c_ref[rows, cols] = c_ref[rows, cols] - dot_nt(m_ref[rows, block(k)], c_ref[cols, block(k)])


    def fill_one(h, j):
        shared = u_ref[pl.ds(pl.multiple_of(256 * pair, 256), 256), 384 * h + 128 * j : 384 * h + 128 * j + 128]
        base = 192 + 32 * (3 * h + j)
        other = jnp.concatenate(
            [bulk_ref[8 * pair + k, base : base + 32] for k in range(8)], 0
        )
        left = jnp.concatenate([left_ref[0], left_ref[1]], 0)
        both = dot(left, jnp.concatenate([shared, other], 1), MID)
        halves = join_pair(both[:, 0:128], both[:, 128:256])
        at = 256 * j
        cols = slice(768 * h + at, 768 * h + at + 256)
        rows = []
        for t in range(2):
            part = jnp.concatenate([half[96 * t : 96 * t + 96] for half in halves], 1)
            if t == h:
                natural = jnp.where(
                    first == (t == 0),
                    mine_ref[32:128, 256 + at : 512 + at],
                    recv_ref[32:128, 256 + at : 512 + at],
                )
                rows.append(natural - part)
            else:
                rows.append(-part)
        one_ref[:, cols], one_send_ref[:, cols] = choose(first, rows[0], rows[1])

    def wait_late():
        for copy in copies[1]:
            copy.wait()

    def fill_l(p, t):
        for k in range(8):
            for j in range(3):
                base = 384 + 144 * t + 48 * j
                l_ref[2 * p + t, 48 * k : 48 * k + 48, 128 * j : 128 * j + 128] = bulk_ref[
                    8 * p + k, base : base + 48
                ]
                base = 192 + 32 * (3 * t + j)
                l_ref[2 * p + t, 384 + 32 * k : 416 + 32 * k, 128 * j : 128 * j + 128] = bulk_ref[
                    8 * p + k, base : base + 32
                ]

    inverse = []
    extra = slice(512, 608)
    run = functools.partial
    work = [
        [run(fill_v, rest, t) for t in range(2)]
        + [run(fill_ut, i) for i in (1, 2, 3)]
        + [fill_rest, fill_f],
        [
            run(side, 0, slice(256, 608)),
            run(trail, 0, block(2), 1, 3),
            run(trail, 0, block(3), 1, 4),
            run(trail, 0, extra, 1, 4),
            wait_late,
        ]
        + [run(fill_one, 0, j) for j in range(3)],
        [
            run(side, 1, slice(384, 608)),
            run(trail, 1, block(3), 2, 4),
            run(trail, 1, extra, 2, 4),
        ]
        + [run(fill_one, 1, j) for j in range(3)],
        [
            run(side, 2, extra),
            run(trail, 2, extra, 3, 4),
        ]
        + [run(fill_l, p, t) for p in range(2) for t in range(2)],
    ]
    for t in range(2):
        fill_v(head, t)
    fill_ut(0)
    fill_c(head, 128)
    c_ref[head, head] = c_ref[head, head] + s1_ref[0, head, head]
    for k in range(4):
        if k:
            side(k - 1, block(k))
            trail(k - 1, block(k), k, k + 1)
        (x,) = sweep_blocks([c_ref[block(k), block(k)]], work[k])
        inverse.append(-x)
    g = [None] * 4
    total = t_ref[...]
    g[3] = dot(c_ref[extra, block(3)], inverse[3])
    for k in (2, 1, 0):
        total = total - dot(g[k + 1], v_ref[block(k + 1), :], MID)
        after = jnp.concatenate(g[k + 1 :], 1)
        g[k] = m_ref[extra, block(k)] - dot(after, m_ref[128 * (k + 1) : 512, block(k)])
    total = total - dot(g[0], v_ref[block(0), :], MID)
    none = jnp.zeros((48, 384), jnp.float32)
    for p in range(2):
        for t in range(2):
            weights = jnp.concatenate([total[:, 384 * t : 384 * t + 384], g[2 * p], g[2 * p + 1]], 1)
            own = jnp.where(pair == p, lee_ref[t], 0.0)
            placed = jnp.concatenate([own, none] if t == 0 else [none, own], 0)
            out = placed - dot(weights, l_ref[2 * p + t], MID)
            cols = slice(384 * (2 * p + t), 384 * (2 * p + t) + 384)
            two_ref[:, cols], two_send_ref[:, cols] = choose(first, out[0:48], out[48:96])


def call(kernel, outs, args, micros, limit, scratch=(), scalars=True, hbm=0):
    shapes = [jax.ShapeDtypeStruct(s, jnp.float32) for s in outs]
    specs = [pl.BlockSpec(memory_space=pltpu.SMEM)] if scalars else []
    specs += [pl.BlockSpec(memory_space=pltpu.HBM)] * hbm
    specs += [pl.BlockSpec(memory_space=pltpu.VMEM)] * (len(args) - len(specs))
    return pl.pallas_call(
        kernel,
        out_shape=shapes,
        in_specs=specs,
        out_specs=[pl.BlockSpec(memory_space=pltpu.VMEM) for _ in outs],
        scratch_shapes=scratch,
        compiler_params=pltpu.CompilerParams(vmem_limit_bytes=limit * 2**20),
        cost_estimate=pl.CostEstimate(
            flops=int(micros * 1e9), bytes_accessed=2**20, transcendentals=0
        ),
    )(*args)


def swap(x, axis):
    return lax.ppermute(x, axis, [(0, 1), (1, 0)])


def by_slot(core, mine, other):
    first = core == 0
    return jnp.stack([jnp.where(first, mine, other), jnp.where(first, other, mine)])[:, None]


def floats(*shape):
    return pltpu.VMEM(shape, jnp.float32)


def damped(rows, offset, gain):
    count, width = rows.shape
    row = lax.broadcasted_iota(jnp.int32, (count, width), 0) + offset
    lane = lax.broadcasted_iota(jnp.int32, (count, width), 1)
    return rows + jnp.where(row == lane, gain[None, :], 0.0)


def shift_by(x, axis, step):
    return lax.ppermute(x, axis, [(i, (i + step) % 4) for i in range(4)])


def local(interface_rows, exterior_rows, pml_mask):
    core = lax.axis_index("core")
    blk = lax.axis_index(("xl", "z"))
    where = jnp.stack(
        [core, blk, lax.axis_index("xh"), lax.axis_index(("xh", "xl")), lax.axis_index("z")]
    ).astype(jnp.int32)

    def slot_rows(second):
        slots = []
        for s in range(2):
            gain = DAMPING * pml_mask[s, 0].astype(jnp.float32)
            slots.append(
                jnp.concatenate(
                    [
                        damped(interface_rows[s, 0], blk * 32, gain),
                        damped(exterior_rows[s, 0], 256 + blk * 96, gain),
                    ],
                    0,
                )
            )
        return jnp.where(second, slots[1], slots[0])

    send = slot_rows(core == 0)
    recv = swap(send, "core")
    mine = slot_rows(core == 1)
    keep, away, s1, bulk, es, ei, lee = call(
        split_kernel,
        [
            (2, 48, 128),
            (2, 48, 128),
            (2, 32, 128),
            (672, 128),
            (2, 48, 384),
            (2, 48, 256),
            (2, 48, 384),
        ],
        [where, mine, recv],
        2,
        8,
    )
    bulk_all = lax.all_gather(bulk, PLANE, axis=0, tiled=False)
    shared = keep + swap(away, "xh")
    early = jnp.concatenate([shared.reshape(96, 128), s1.reshape(64, 128)], 0)
    line = jnp.stack([early] + [shift_by(early, ("xh", "xl"), d) for d in (1, 2, 3)])
    plane = [line] + [shift_by(line, "z", d) for d in (1, 2, 3)]
    early_outs = call(
        first_kernel,
        [(2, 432, 384), (2, 256, 256), (2, 96, 256)],
        [where, *plane, mine, recv, es],
        20,
        12,
        scratch=[floats(256, 256), floats(2, 384, 256)],
    )
    one, one_send, two, two_send = call(
        late_kernel,
        [(96, 1536), (96, 1536), (48, 1536), (48, 1536)],
        [where, bulk_all, *early_outs, ei, lee, mine, recv],
        25,
        48,
        hbm=1,
        scratch=[
            floats(512, 768),
            floats(768, 512),
            floats(512, 768),
            floats(608, 512),
            floats(608, 512),
            floats(4, 640, 384),
            floats(96, 768),
            floats(16, 672, 128),
            pltpu.SemaphoreType.DMA((32,)),
        ],
    )
    one_recv = swap(one_send, "core")
    two_recv = swap(two_send, "core")
    return by_slot(core, one, one_recv), by_slot(core, two, two_recv)


def solution(mesh):
    fine = Mesh(mesh.devices.reshape(4, 2, 2, 2, 4), ("y", "xh", "core", "xl", "z"))
    box, blk = ("y", "xh", "core"), ("xl", "z")
    rows = P(None, box, blk, None)
    return jax.shard_map(
        local,
        mesh=fine,
        in_specs=(rows, rows, P(None, box, None)),
        out_specs=(rows, rows),
        check_vma=False,
    )
```

```python
import functools

import jax
import jax.numpy as jnp
from jax import lax
from jax.experimental import pallas as pl
from jax.experimental.pallas import tpu as pltpu
from jax.sharding import Mesh
from jax.sharding import PartitionSpec as P

HI = lax.Precision.HIGHEST
MID = lax.Precision.HIGH
DAMPING = 2.0
PLANE = ("xh", "xl", "z")


def dot(a, b, precision=HI):
    return jnp.dot(a, b, precision=precision, preferred_element_type=jnp.float32)


def dot_nt(a, b, precision=HI):
    return lax.dot_general(
        a, b, (((1,), (1,)), ((), ())), precision=precision, preferred_element_type=jnp.float32
    )


def dot_tn(a, b):
    return lax.dot_general(
        a, b, (((0,), (0,)), ((), ())), precision=HI, preferred_element_type=jnp.float32
    )


PANEL = 16


def tree_sum(t):
    while len(t) > 1:
        t = [t[i] + t[i + 1] for i in range(0, len(t) - 1, 2)] + ([t[-1]] if len(t) % 2 else [])
    return t[0]


def spread_lane(x, at):
    return jnp.broadcast_to(x[:, at : at + 1], x.shape)


def spread_row(x, at):
    return jnp.broadcast_to(x[at : at + 1], x.shape)


def eliminate(rows, base, lane, sub):
    count = 8 * len(rows)
    cols = [[spread_lane(x, base + q) for x in rows] for q in range(count)]
    inblk = (lane >= base) & (lane < base + count)
    out = [
        jnp.where(inblk, jnp.where(lane == sub + (8 * v + base), -1.0, 0.0), x)
        for v, x in enumerate(rows)
    ]
    scale = 1.0 / spread_row(cols[0][0], 0)
    for k in range(count):
        kv, ks = divmod(k, 8)
        hit = sub == ks
        if k + 1 < count:
            nv, ns = divmod(k + 1, 8)
            over = spread_row(cols[k + 1][kv], ks) * scale
            pivot = spread_row(cols[k + 1][nv], ns) - spread_row(cols[k][nv], ns) * over
            ahead = 1.0 / pivot

        def update(tiles):
            row = spread_row(tiles[kv], ks) * scale
            new = [x - c * row for x, c in zip(tiles, cols[k])]
            new[kv] = jnp.where(hit, row, new[kv])
            return new

        for j in range(k + 1, count):
            cols[j] = update(cols[j])
        out = update(out)
        if k + 1 < count:
            scale = ahead
    return out


def sweep_blocks(mats, work=()):
    work = list(work)
    tiles, per = 16, PANEL // 8
    lane = lax.broadcasted_iota(jnp.int32, (8, 128), 1)
    sub = lax.broadcasted_iota(jnp.int32, (8, 128), 0)
    mats = [[a[8 * i : 8 * i + 8] for i in range(tiles)] for a in mats]
    for k in range(tiles // per):
        base = PANEL * k
        inblk = (lane >= base) & (lane < base + PANEL)
        own = range(per * k, per * k + per)
        near = range(per * k + per, min(per * k + 2 * per, tiles))
        for c, rows in enumerate(mats):
            cols = {t: [spread_lane(rows[t], base + q) for q in range(PANEL)] for t in near}
            solved = eliminate([rows[t] for t in own], base, lane, sub)
            new = list(rows)
            if near:
                each = [spread_row(solved[q // 8], q % 8) for q in range(PANEL)]
                for t in near:
                    total = tree_sum([cols[t][q] * each[q] for q in range(PANEL)])
                    new[t] = jnp.where(inblk, 0.0, rows[t]) - total
            change = dot_tn(
                jnp.concatenate([rows[t] for t in own], 0), jnp.concatenate(solved, 0)
            )
            for t in range(tiles):
                if t in own:
                    new[t] = solved[t - per * k]
                elif t not in near:
                    new[t] = jnp.where(inblk, 0.0, rows[t]) - change[8 * t : 8 * t + 8]
            mats[c] = new
        left = tiles // per - k
        for _ in range(-(-len(work) // left)):
            work.pop(0)()
    return [jnp.concatenate(rows, 0) for rows in mats]


def lane_index(rows, back):
    lane = lax.broadcasted_iota(jnp.int32, (rows, 128), 1)
    if back:
        seg = lane // 16
        return (seg % 2) * 64 + (seg // 2) * 16 + lane % 16
    half = lane // 64
    return ((lane % 64) // 16) * 32 + half * 16 + lane % 16


def pick(x, index):
    return jnp.take_along_axis(x, index, axis=1)


def split_columns(x):
    rows = x.shape[0]
    index = lane_index(rows, False)
    low = lax.broadcasted_iota(jnp.int32, (rows, 128), 1) < 64
    shared, other = [], []
    for j in range(3):
        a = pick(x[:, 256 * j : 256 * j + 128], index)
        b = pick(x[:, 256 * j + 128 : 256 * j + 256], index)
        shared.append(jnp.where(low, a, pltpu.roll(b, 64, 1)))
        other.append(jnp.where(low, pltpu.roll(a, 64, 1), b))
    return shared + other


def join_pair(shared, other):
    rows = shared.shape[0]
    index = lane_index(rows, True)
    low = lax.broadcasted_iota(jnp.int32, (rows, 128), 1) < 64
    return (
        pick(jnp.where(low, shared, pltpu.roll(other, 64, 1)), index),
        pick(jnp.where(low, pltpu.roll(shared, 64, 1), other), index),
    )


def shared_rows(x):
    return jnp.concatenate([x[0:16], x[32:48], x[64:80]], 0)


def other_rows(x):
    return jnp.concatenate([x[16:32], x[48:64], x[80:96]], 0)


def choose(first, a, b):
    return jnp.where(first, a, b), jnp.where(first, b, a)


def split_kernel(
    where_ref, mine_ref, recv_ref, keep_ref, send_ref, s1_ref, bulk_ref, es_ref, ei_ref, lee_ref
):
    first = where_ref[0] == 0
    upper = where_ref[2] == 0
    boxes = choose(first, mine_ref[...], recv_ref[...])
    total = boxes[0][0:32, 0:256] + boxes[1][0:32, 0:256]
    s1_ref[0] = total[:, 0:128]
    s1_ref[1] = total[:, 128:256]
    kept = []
    blocks = [(where_ref[1] * 48 + 16 * s) // 128 for s in range(3)]
    for t, box in enumerate(boxes):
        panels = split_columns(box[:, 256:1024])
        for j in range(6):
            base = 32 * (3 * t + j % 3) + 192 * (j // 3)
            bulk_ref[base : base + 32, :] = panels[j][0:32]
        for j in range(3):
            base = 384 + 144 * t + 48 * j
            bulk_ref[base : base + 48, :] = shared_rows(panels[3 + j][32:128])
            es_ref[t, :, 128 * j : 128 * j + 128] = other_rows(panels[j][32:128])
            lee_ref[t, :, 128 * j : 128 * j + 128] = other_rows(panels[3 + j][32:128])
        ei_ref[t] = other_rows(box[32:128, 0:256])
        kept.append([shared_rows(panels[j][32:128]) for j in range(3)])
    for s, i in enumerate(blocks):
        rows = slice(16 * s, 16 * s + 16)
        for step in range(2):
            tiles = []
            for t in range(2):
                a, b, c = (kept[t][(j + step) % 3][rows] for j in range(3))
                tiles.append(jnp.where(i == 0, a, jnp.where(i == 1, b, c)))
            keep_ref[step, rows], send_ref[step, rows] = choose(upper, *tiles)


def first_kernel(
    where_ref,
    x0_ref,
    x1_ref,
    x2_ref,
    x3_ref,
    mine_ref,
    recv_ref,
    es_ref,
    dd_ref,
    s1_ref,
    s_ref,
    e_ref,
):
    first = where_ref[0] == 0
    pair, x, z = where_ref[2], where_ref[3], where_ref[4]
    d_ref, direct_ref = dd_ref.at[:, 0:384], dd_ref.at[:, 384:432]
    left_ref = dd_ref.at[:, 432:528, 0:256]
    for turn, ref in enumerate((x0_ref, x1_ref, x2_ref, x3_ref)):
        for shift in range(4):
            source = lax.rem(x + 4 - shift, 4)
            half, low = source // 2, lax.rem(source, 2)
            k = low * 4 + lax.rem(z + 4 - turn, 4)
            rows = pl.ds(pl.multiple_of(48 * k, 16), 48)
            for j in range(2):
                e_ref[half, rows, 128 * j : 128 * j + 128] = ref[shift, 48 * j : 48 * j + 48]
            rows = pl.ds(pl.multiple_of(32 * k, 32), 32)
            for j in range(2):
                s1_ref[half, rows, 128 * j : 128 * j + 128] = ref[
                    shift, 96 + 32 * j : 128 + 32 * j
                ]
    s_ref[...] = s1_ref[pair]
    mats = [e_ref.at[0], e_ref.at[1], s_ref]
    both = range(2)

    def at(i, j):
        return slice(128 * i, 128 * i + 128), slice(128 * j, 128 * j + 128)

    def inverses(blocks, work=()):
        return [-x for x in sweep_blocks(blocks, work)]

    x0 = inverses([ref[at(0, 0)] for ref in mats])
    a01 = [ref[at(0, 1)] for ref in mats]
    m1 = [dot_tn(a, x) for a, x in zip(a01, x0)]
    corners = [ref[at(1, 0)] for ref in mats[:2]] + [s_ref[at(1, 1)]]
    a11 = [c - dot(m, a) for c, m, a in zip(corners, m1, a01)]
    m2, a21, a22, p2, b00, b10 = ([None] * 2 for _ in range(6))

    def third_rows(c):
        a20 = mats[c][at(2, 1)]
        m2[c] = dot(a20, x0[c])
        a21[c] = mats[c][at(1, 1)].T - dot(m2[c], a01[c])
        a22[c] = mats[c][at(2, 0)] - dot_nt(m2[c], a20)

    x1 = inverses(a11, [functools.partial(third_rows, c) for c in both])
    n2 = [dot(a21[c], x1[c]) for c in both]
    last = [a22[c] - dot_nt(n2[c], a21[c]) for c in both]

    def two_by_two(c):
        q = dot(x1[c], m1[c])
        return x0[c] + dot_tn(m1[c], q), -q

    def corner(c):
        p2[c] = m2[c] - dot(n2[c], m1[c])
        b00[c], b10[c] = two_by_two(c)

    def interface():
        s00, s10 = two_by_two(2)
        s_ref[at(0, 0)] = s00
        s_ref[at(1, 0)] = s10
        s_ref[at(0, 1)] = s10.T
        s_ref[at(1, 1)] = x1[2]

    def weights():
        boxes = choose(first, mine_ref[32:128, 0:256], recv_ref[32:128, 0:256])
        for t in range(2):
            left_ref[t] = dot(boxes[t], s_ref[...])

    x2 = inverses(last, [functools.partial(corner, c) for c in both] + [interface, weights])
    for c in both:
        ref = d_ref.at[c]
        q0, q1 = dot(x2[c], p2[c]), dot(x2[c], n2[c])
        mid = b10[c] + dot_tn(n2[c], q0)
        ref[at(0, 0)] = b00[c] + dot_tn(p2[c], q0)
        ref[at(1, 0)] = mid
        ref[at(0, 1)] = mid.T
        ref[at(1, 1)] = x1[c] + dot_tn(n2[c], q1)
        ref[at(2, 0)] = -q0
        ref[at(0, 2)] = -q0.T
        ref[at(2, 1)] = -q1
        ref[at(1, 2)] = -q1.T
        ref[at(2, 2)] = x2[c]
        direct_ref[c] = dot(es_ref[c], ref[...])


def late_kernel(
    where_ref,
    bulk_hbm,
    dd_ref,
    s1_ref,
    ei_ref,
    lee_ref,
    mine_ref,
    recv_ref,
    one_ref,
    one_send_ref,
    two_ref,
    two_send_ref,
    u_ref,
    ut_ref,
    v_ref,
    c_ref,
    m_ref,
    l_ref,
    t_ref,
    bulk_ref,
    sems,
):
    first = where_ref[0] == 0
    upper = where_ref[2] == 0
    pair = where_ref[2]
    d_ref, direct_ref = dd_ref.at[:, 0:384], dd_ref.at[:, 384:432]
    left_ref = dd_ref.at[:, 432:528, 0:256]
    parts = (slice(0, 192), slice(192, 672))
    copies = [
        [
            pltpu.make_async_copy(
                bulk_hbm.at[i, part], bulk_ref.at[i, part], sems.at[16 * h + i]
            )
            for i in range(16)
        ]
        for h, part in enumerate(parts)
    ]
    for group in copies:
        for copy in group:
            copy.start()
    for copy in copies[0]:
        copy.wait()

    def block(i):
        return slice(128 * i, 128 * i + 128)

    for p in range(2):
        for k in range(8):
            at = slice(256 * p + 32 * k, 256 * p + 32 * k + 32)
            for t in range(2):
                for j in range(3):
                    base = 32 * (3 * t + j)
                    u_ref[at, 384 * t + 128 * j : 384 * t + 128 * j + 128] = bulk_ref[
                        8 * p + k, base : base + 32
                    ]


    head, rest = slice(0, 128), slice(128, 512)

    def fill_v(rows, t):
        cols = slice(384 * t, 384 * t + 384)
        v_ref[rows, cols] = dot(u_ref[rows, cols], d_ref[t])

    def fill_ut(i):
        ut_ref[:, block(i)] = u_ref[block(i), :].T

    def fill_c(rows, width):
        c_ref[rows, 0:width] = -dot(v_ref[rows, :], ut_ref[:, 0:width], MID)

    def add_s1(rows, p):
        cols = slice(256 * p, 256 * p + 256)
        start = rows.start - 256 * p
        c_ref[rows, cols] = c_ref[rows, cols] + s1_ref[p, start : start + rows.stop - rows.start, :]

    def fill_f():
        blank = jnp.zeros((48, 256), jnp.float32)
        none = jnp.zeros((48, 384), jnp.float32)
        for t in range(2):
            rows, cols = slice(48 * t, 48 * t + 48), slice(384 * t, 384 * t + 384)
            placed = jnp.concatenate(choose(upper, ei_ref[t], blank), 1)
            c_ref[512 + 48 * t : 560 + 48 * t, :] = placed - dot(
                direct_ref[t], ut_ref[cols, :], MID
            )
            t_ref[rows, cols] = direct_ref[t]
            t_ref[rows, 384 - 384 * t : 768 - 384 * t] = none

    def fill_rest():
        fill_c(rest, 512)
        add_s1(slice(128, 256), 0)
        add_s1(slice(256, 512), 1)

    def side(k, rows):
        m_ref[rows, block(k)] = dot(c_ref[rows, block(k)], inverse[k])

    def trail(k, rows, start, stop):
        cols = slice(128 * start, 128 * stop)
        c_ref[rows, cols] = c_ref[rows, cols] - dot_nt(m_ref[rows, block(k)], c_ref[cols, block(k)])


    def fill_one(h, j):
        shared = u_ref[pl.ds(pl.multiple_of(256 * pair, 256), 256), 384 * h + 128 * j : 384 * h + 128 * j + 128]
        base = 192 + 32 * (3 * h + j)
        other = jnp.concatenate(
            [bulk_ref[8 * pair + k, base : base + 32] for k in range(8)], 0
        )
        left = jnp.concatenate([left_ref[0], left_ref[1]], 0)
        both = dot(left, jnp.concatenate([shared, other], 1), MID)
        halves = join_pair(both[:, 0:128], both[:, 128:256])
        at = 256 * j
        cols = slice(768 * h + at, 768 * h + at + 256)
        rows = []
        for t in range(2):
            part = jnp.concatenate([half[96 * t : 96 * t + 96] for half in halves], 1)
            if t == h:
                natural = jnp.where(
                    first == (t == 0),
                    mine_ref[32:128, 256 + at : 512 + at],
                    recv_ref[32:128, 256 + at : 512 + at],
                )
                rows.append(natural - part)
            else:
                rows.append(-part)
        one_ref[:, cols], one_send_ref[:, cols] = choose(first, rows[0], rows[1])

    def wait_late():
        for copy in copies[1]:
            copy.wait()

    def fill_l(p, t):
        for k in range(8):
            for j in range(3):
                base = 384 + 144 * t + 48 * j
                l_ref[2 * p + t, 48 * k : 48 * k + 48, 128 * j : 128 * j + 128] = bulk_ref[
                    8 * p + k, base : base + 48
                ]
                base = 192 + 32 * (3 * t + j)
                l_ref[2 * p + t, 384 + 32 * k : 416 + 32 * k, 128 * j : 128 * j + 128] = bulk_ref[
                    8 * p + k, base : base + 32
                ]

    inverse = []
    extra = slice(512, 608)
    run = functools.partial
    work = [
        [run(fill_v, rest, t) for t in range(2)]
        + [run(fill_ut, i) for i in (1, 2, 3)]
        + [fill_rest, fill_f],
        [
            run(side, 0, slice(256, 608)),
            run(trail, 0, block(2), 1, 3),
            run(trail, 0, block(3), 1, 4),
            run(trail, 0, extra, 1, 4),
            wait_late,
        ]
        + [run(fill_one, 0, j) for j in range(3)],
        [
            run(side, 1, slice(384, 608)),
            run(trail, 1, block(3), 2, 4),
            run(trail, 1, extra, 2, 4),
        ]
        + [run(fill_one, 1, j) for j in range(3)],
        [
            run(side, 2, extra),
            run(trail, 2, extra, 3, 4),
        ]
        + [run(fill_l, p, t) for p in range(2) for t in range(2)],
    ]
    for t in range(2):
        fill_v(head, t)
    fill_ut(0)
    fill_c(head, 128)
    c_ref[head, head] = c_ref[head, head] + s1_ref[0, head, head]
    for k in range(4):
        if k:
            side(k - 1, block(k))
            trail(k - 1, block(k), k, k + 1)
        (x,) = sweep_blocks([c_ref[block(k), block(k)]], work[k])
        inverse.append(-x)
    g = [None] * 4
    total = t_ref[...]
    g[3] = dot(c_ref[extra, block(3)], inverse[3])
    for k in (2, 1, 0):
        total = total - dot(g[k + 1], v_ref[block(k + 1), :], MID)
        after = jnp.concatenate(g[k + 1 :], 1)
        g[k] = m_ref[extra, block(k)] - dot(after, m_ref[128 * (k + 1) : 512, block(k)])
    total = total - dot(g[0], v_ref[block(0), :], MID)
    none = jnp.zeros((48, 384), jnp.float32)
    for p in range(2):
        for t in range(2):
            weights = jnp.concatenate([total[:, 384 * t : 384 * t + 384], g[2 * p], g[2 * p + 1]], 1)
            own = jnp.where(pair == p, lee_ref[t], 0.0)
            placed = jnp.concatenate([own, none] if t == 0 else [none, own], 0)
            out = placed - dot(weights, l_ref[2 * p + t], MID)
            cols = slice(384 * (2 * p + t), 384 * (2 * p + t) + 384)
            two_ref[:, cols], two_send_ref[:, cols] = choose(first, out[0:48], out[48:96])


def call(kernel, outs, args, micros, limit, scratch=(), scalars=True, hbm=0):
    shapes = [jax.ShapeDtypeStruct(s, jnp.float32) for s in outs]
    specs = [pl.BlockSpec(memory_space=pltpu.SMEM)] if scalars else []
    specs += [pl.BlockSpec(memory_space=pltpu.HBM)] * hbm
    specs += [pl.BlockSpec(memory_space=pltpu.VMEM)] * (len(args) - len(specs))
    return pl.pallas_call(
        kernel,
        out_shape=shapes,
        in_specs=specs,
        out_specs=[pl.BlockSpec(memory_space=pltpu.VMEM) for _ in outs],
        scratch_shapes=scratch,
        compiler_params=pltpu.CompilerParams(vmem_limit_bytes=limit * 2**20),
        cost_estimate=pl.CostEstimate(
            flops=int(micros * 1e9), bytes_accessed=2**20, transcendentals=0
        ),
    )(*args)


def swap(x, axis):
    return lax.ppermute(x, axis, [(0, 1), (1, 0)])


def by_slot(core, mine, other):
    first = core == 0
    return jnp.stack([jnp.where(first, mine, other), jnp.where(first, other, mine)])[:, None]


def floats(*shape):
    return pltpu.VMEM(shape, jnp.float32)


def damped(rows, offset, gain):
    count, width = rows.shape
    row = lax.broadcasted_iota(jnp.int32, (count, width), 0) + offset
    lane = lax.broadcasted_iota(jnp.int32, (count, width), 1)
    return rows + jnp.where(row == lane, gain[None, :], 0.0)


def shift_by(x, axis, step):
    return lax.ppermute(x, axis, [(i, (i + step) % 4) for i in range(4)])


def local(interface_rows, exterior_rows, pml_mask):
    core = lax.axis_index("core")
    blk = lax.axis_index(("xl", "z"))
    where = jnp.stack(
        [core, blk, lax.axis_index("xh"), lax.axis_index(("xh", "xl")), lax.axis_index("z")]
    ).astype(jnp.int32)

    def slot_rows(second):
        slots = []
        for s in range(2):
            gain = DAMPING * pml_mask[s, 0].astype(jnp.float32)
            slots.append(
                jnp.concatenate(
                    [
                        damped(interface_rows[s, 0], blk * 32, gain),
                        damped(exterior_rows[s, 0], 256 + blk * 96, gain),
                    ],
                    0,
                )
            )
        return jnp.where(second, slots[1], slots[0])

    send = slot_rows(core == 0)
    recv = swap(send, "core")
    mine = slot_rows(core == 1)
    keep, away, s1, bulk, es, ei, lee = call(
        split_kernel,
        [
            (2, 48, 128),
            (2, 48, 128),
            (2, 32, 128),
            (672, 128),
            (2, 48, 384),
            (2, 48, 256),
            (2, 48, 384),
        ],
        [where, mine, recv],
        2,
        8,
    )
    bulk_all = lax.all_gather(bulk, PLANE, axis=0, tiled=False)
    shared = keep + swap(away, "xh")
    early = jnp.concatenate([shared.reshape(96, 128), s1.reshape(64, 128)], 0)
    line = jnp.stack([early] + [shift_by(early, ("xh", "xl"), d) for d in (1, 2, 3)])
    plane = [line] + [shift_by(line, "z", d) for d in (1, 2, 3)]
    early_outs = call(
        first_kernel,
        [(2, 528, 384), (2, 256, 256)],
        [where, *plane, mine, recv, es],
        20,
        12,
        scratch=[floats(256, 256), floats(2, 384, 256)],
    )
    one, one_send, two, two_send = call(
        late_kernel,
        [(96, 1536), (96, 1536), (48, 1536), (48, 1536)],
        [where, bulk_all, *early_outs, ei, lee, mine, recv],
        25,
        46,
        hbm=1,
        scratch=[
            floats(512, 768),
            floats(768, 512),
            floats(512, 768),
            floats(608, 512),
            floats(608, 512),
            floats(4, 640, 384),
            floats(96, 768),
            floats(16, 672, 128),
            pltpu.SemaphoreType.DMA((32,)),
        ],
    )
    one_recv = swap(one_send, "core")
    two_recv = swap(two_send, "core")
    return by_slot(core, one, one_recv), by_slot(core, two, two_recv)


def solution(mesh):
    fine = Mesh(mesh.devices.reshape(4, 2, 2, 2, 4), ("y", "xh", "core", "xl", "z"))
    box, blk = ("y", "xh", "core"), ("xl", "z")
    rows = P(None, box, blk, None)
    return jax.shard_map(
        local,
        mesh=fine,
        in_specs=(rows, rows, P(None, box, None)),
        out_specs=(rows, rows),
        check_vma=False,
    )
```
